32 devices in a mesh: space: 8 (over z, y), tile: 4 (over x, core).
Axes of the slice: x: 2, y: 2, z: 4, core: 2. Of those that a mesh axis runs over, the one named last changes fastest.
Arguments:
- features: bfloat16 [8, 4, 64, 8, 8, 256], P('space', 'tile'), may hold values from -6 to 6
- weight: bfloat16 [3, 3, 3, 32, 32], replicated, may hold values from -0.21875 to 0.21875
- bias_vector: float32 [32], replicated, may hold values from -4 to 4
- cotangent: bfloat16 [8, 4, 64, 8, 8, 256], P('space', 'tile'), may hold values from -6 to 6
- counts: int32 [8, 4], P('space', 'tile'), may hold values from 8 to 64, as said below
- send_slots: int32 [8, 4, 8, 16], P('space', 'tile'), may hold values from 0 to 63
- neighbours: int32 [8, 4, 64, 26], P('space', 'tile'), may hold values from 0 to 192, as said below
Outputs:
- output: bfloat16 [8, 4, 64, 8, 8, 256], P('space', 'tile')
- input_grad: bfloat16 [8, 4, 64, 8, 8, 256], P('space', 'tile')
- weight_grad: float32 [3, 3, 3, 32, 32], replicated
- bias_grad: float32 [32], replicated
The draws below stay inside these ranges and needn't reach their ends.
Inputs may be any that keep to these rules, and one draw needn't show every extreme that they name: `counts`: some device has all 64 slots active in every draw. `send_slots`: slots may repeat and may name inactive slots. `neighbours`: indices below 64 are the device's own slots, the next 128 its imported bricks in direction order, and 192 the zero brick, which some entry names in every draw.
All inputs are finite; a program needn't handle non-finite values.
Results may differ from the reference program's by a relative error of at most 0.0019.
Values may be sent and summed in bfloat16 or wider, within the bound.
No kernel may reach another device: no remote copies, remote signals or barrier semaphores. Data moves between devices by JAX's collectives and lax.ppermute only.
A program may use at most 256 MiB of HBM per device.

```python
import jax
import jax.numpy as jnp
import numpy as np
from jax import lax

C = 32
BCAP = 64
KSLOT = 16
N_SPACE = 8
N_TILE = 4


def draw_counts(key, part):
    key = jax.random.fold_in(key, 11)
    first_key, second_key, third_key = jax.random.split(key, 3)
    lowest = max(1, BCAP // 8)
    base = jax.random.randint(first_key, (N_SPACE, N_TILE), lowest, BCAP // 2 + 1)
    filled = jax.random.randint(second_key, (N_SPACE, N_TILE), 0, 8) == 0
    chosen = jax.random.randint(third_key, (), 0, N_SPACE * N_TILE)
    flat_ids = jnp.arange(N_SPACE * N_TILE, dtype=jnp.int32).reshape(N_SPACE, N_TILE)
    filled = filled | (flat_ids == chosen)
    return jnp.where(filled, BCAP, base).astype(jnp.int32)


def draw_neighbours(key, part):
    key = jax.random.fold_in(key, 23)
    kind_key, local_key, import_key, place_key = jax.random.split(key, 4)
    shape_all = (N_SPACE, N_TILE, BCAP, 26)
    kinds = jax.random.randint(kind_key, shape_all, 0, 20)
    local_ids = jax.random.randint(local_key, shape_all, 0, BCAP)
    import_ids = jax.random.randint(import_key, shape_all, BCAP, BCAP + 8 * KSLOT)
    empty_id = BCAP + 8 * KSLOT
    result = jnp.where(kinds < 12, local_ids, jnp.where(kinds < 17, import_ids, empty_id))
    placed = jax.random.randint(place_key, (), 0, 26)
    corner = jnp.arange(26, dtype=jnp.int32) == placed
    result = result.at[0, 0, 0].set(jnp.where(corner, empty_id, result[0, 0, 0]))
    return result.astype(jnp.int32)


def plant(array, rng, least, top_value):
    longest = array.shape.index(max(array.shape))
    spots = []
    for shift in (0, 1):
        where = [jax.random.randint(jax.random.fold_in(rng, axis), (), 0, length) for axis, length in enumerate(array.shape)]
        where[longest] = (where[longest] + shift) % array.shape[longest]
        spots.append(tuple(where))
    return array.at[spots[0]].set(least).at[spots[1]].set(top_value)


def shard_levels(stream_key, dims, cuts, smallest, high):
    def one(position, shards_of):
        draws = jax.random.uniform(jax.random.fold_in(jax.random.fold_in(stream_key, 6), position), (shards_of,), jnp.float32, smallest / len(cuts), high / len(cuts))
        return jnp.repeat(jnp.exp(draws), dims[position] // shards_of).reshape((-1,) + (1,) * (len(dims) - position - 1))

    gain = one(*cuts[0])
    for cut in cuts[1:]:
        gain = gain * one(*cut)
    return gain


def normal_values(rng, dims, scale, limit, cuts=(), kind=jnp.bfloat16):
    array = scale * jax.random.normal(rng, dims, jnp.float32)
    if cuts:
        array = array * shard_levels(rng, dims, cuts, -0.22, 0.18)
    return jnp.clip(array, -limit, limit).astype(kind)


def setup_inputs(seed: int = 0) -> dict:
    key_list = jax.random.split(jax.random.key(seed), 8)
    features = normal_values(key_list[0], (N_SPACE, N_TILE, BCAP, 8, 8, 8 * C), 1.0, 6.0, ((0, 8), (1, 4)))
    weight = normal_values(key_list[1], (3, 3, 3, C, C), (27 * C) ** -0.5, 0.21875)
    bias_vector = normal_values(key_list[2], (C,), 1.0, 4.0, (), jnp.float32)
    cotangent = normal_values(key_list[3], (N_SPACE, N_TILE, BCAP, 8, 8, 8 * C), 1.0, 6.0, ((0, 8), (1, 4)))
    counts = draw_counts(jax.random.fold_in(key_list[7], 71), 0)
    send_slots = plant(jax.random.randint(key_list[5], (N_SPACE, N_TILE, 8, KSLOT), 0, BCAP), jax.random.fold_in(key_list[5], 1), 0, BCAP - 1).astype(jnp.int32)
    neighbours = draw_neighbours(jax.random.fold_in(key_list[7], 71), 0)
    return {"features": features, "weight": weight, "bias_vector": bias_vector, "cotangent": cotangent, "counts": counts, "send_slots": send_slots, "neighbours": neighbours}


NEIGHBOUR_SIDES = [(x_side, y_side, z_side) for x_side in (-1, 0, 1) for y_side in (-1, 0, 1) for z_side in (-1, 0, 1) if (x_side, y_side, z_side) != (0, 0, 0)]
DEVICE_SIDES = [(s_side, t_side) for s_side in (-1, 0, 1) for t_side in (-1, 0, 1) if (s_side, t_side) != (0, 0)]

def side_ranges(side_value):
    if side_value < 0:
        return (7, 8)
    if side_value > 0:
        return (0, 1)
    return (0, 8)

def assemble(own_bricks, near_bricks, channels):
    rows_x = []
    for x_side in (-1, 0, 1):
        rows_y = []
        for y_side in (-1, 0, 1):
            pieces = []
            for z_side in (-1, 0, 1):
                if (x_side, y_side, z_side) == (0, 0, 0):
                    source = own_bricks
                else:
                    source = near_bricks[:, NEIGHBOUR_SIDES.index((x_side, y_side, z_side))]
                x_start, x_stop = side_ranges(x_side)
                y_start, y_stop = side_ranges(y_side)
                z_start, z_stop = side_ranges(z_side)
                pieces.append(source[:, x_start:x_stop, y_start:y_stop, z_start * channels:z_stop * channels])
            rows_y.append(jnp.concatenate(pieces, axis=3))
        rows_x.append(jnp.concatenate(rows_y, axis=2))
    return jnp.concatenate(rows_x, axis=1)

def columns(own_bricks, near_bricks, channels):
    volume = assemble(own_bricks, near_bricks, channels)
    shifted = [volume[:, x_shift:x_shift + 8, y_shift:y_shift + 8, :] for x_shift in range(3) for y_shift in range(3)]
    stacked = jnp.stack(shifted, axis=3)
    return stacked.reshape(own_bricks.shape[0] * 64, 90 * channels)

def band_weights(weight_wide, channels):
    selector = np.zeros((3, 10, 8), np.float32)
    for depth_step in range(3):
        for plane_index in range(8):
            selector[depth_step, plane_index + depth_step, plane_index] = 1.0
    band_matrix = jnp.einsum('kpq,abkio->abpiqo', jnp.asarray(selector, weight_wide.dtype), weight_wide, precision=lax.Precision.HIGHEST)
    return band_matrix.reshape(90 * channels, 8 * channels)

def reference(features, weight, bias_vector, cotangent, counts, send_slots, neighbours):
    channels = weight.shape[-1]
    slot_count = features.shape[2]
    per_side = send_slots.shape[-1]
    row_width = 8 * channels
    device_count = N_SPACE * N_TILE
    active = jnp.arange(slot_count, dtype=jnp.int32)[None, None, :] < counts[:, :, None]
    active_mask = active.astype(jnp.bfloat16)[..., None, None, None]
    masked = features * active_mask
    grads_in = cotangent * active_mask
    band_matrix = band_weights(weight.astype(jnp.float32), channels).astype(jnp.bfloat16)
    bias_row = jnp.tile(bias_vector.astype(jnp.float32), 8)
    zero_brick = jnp.zeros((1, 8, 8, row_width), jnp.bfloat16)

    def imports_of(s_index, t_index):
        blocks = []
        for side_index, (s_side, t_side) in enumerate(DEVICE_SIDES):
            from_s = s_index - s_side
            from_t = t_index - t_side
            inside = (from_s >= 0) & (from_s < N_SPACE) & (from_t >= 0) & (from_t < N_TILE)
            clip_s = jnp.clip(from_s, 0, N_SPACE - 1).astype(jnp.int32)
            clip_t = jnp.clip(from_t, 0, N_TILE - 1).astype(jnp.int32)
            picked = masked[clip_s, clip_t][send_slots[clip_s, clip_t, side_index]]
            blocks.append(picked * inside.astype(jnp.bfloat16))
        return jnp.concatenate(blocks, axis=0)

    def column_map(own_bricks, near_bricks):
        return columns(own_bricks, near_bricks, channels)

    def one_device(state_now, flat_index):
        s_index = flat_index // N_TILE
        t_index = flat_index % N_TILE
        own_bricks = masked[s_index, t_index]
        brick_table = jnp.concatenate([own_bricks, imports_of(s_index, t_index), zero_brick], axis=0)
        near_rows = neighbours[s_index, t_index]
        near_bricks = brick_table[near_rows]
        column_rows = column_map(own_bricks, near_bricks)
        out_sums = jnp.dot(column_rows, band_matrix, preferred_element_type=jnp.float32) + bias_row
        row_mask = jnp.repeat(active[s_index, t_index].astype(jnp.float32), 64)[:, None]
        output_rows = (out_sums * row_mask).astype(jnp.bfloat16).reshape(slot_count, 8, 8, row_width)
        g_rows = grads_in[s_index, t_index].reshape(slot_count * 64, row_width)
        col_grads = lax.dot_general(g_rows, band_matrix, (((1,), (1,)), ((), ())), preferred_element_type=jnp.float32)
        band_grad = lax.dot_general(column_rows, g_rows, (((0,), (0,)), ((), ())), preferred_element_type=jnp.float32)
        bias_grad = lax.optimization_barrier(jnp.sum(g_rows.astype(jnp.float32), axis=0))
        own_zero = jnp.zeros(own_bricks.shape, jnp.float32)
        near_zero = jnp.zeros(near_bricks.shape, jnp.float32)
        unused, pull_back = jax.vjp(column_map, own_zero, near_zero)
        own_grad, near_grad = pull_back(col_grads)
        table_grad = jnp.zeros((slot_count + 8 * per_side + 1, 8, 8, row_width), jnp.float32)
        table_grad = table_grad.at[near_rows.reshape(-1)].add(near_grad.reshape(-1, 8, 8, row_width))
        local_grad = table_grad[:slot_count] + own_grad
        import_grad = table_grad[slot_count:slot_count + 8 * per_side]
        return ((state_now[0] + band_grad, state_now[1] + bias_grad), (output_rows, local_grad, import_grad))
    initial = (jnp.zeros((90 * channels, row_width), jnp.float32), jnp.zeros((row_width,), jnp.float32))
    sums_now, per_device = lax.scan(one_device, initial, jnp.arange(device_count, dtype=jnp.int32))
    band_grad, bias_sum = sums_now
    outputs, local_grads, import_grads = per_device

    def owner_grad(flat_index):
        s_index = flat_index // N_TILE
        t_index = flat_index % N_TILE
        summed = local_grads[flat_index]
        for side_index, (s_side, t_side) in enumerate(DEVICE_SIDES):
            to_s = s_index + s_side
            to_t = t_index + t_side
            inside = (to_s >= 0) & (to_s < N_SPACE) & (to_t >= 0) & (to_t < N_TILE)
            clip_flat = (jnp.clip(to_s, 0, N_SPACE - 1) * N_TILE + jnp.clip(to_t, 0, N_TILE - 1)).astype(jnp.int32)
            import_rows = import_grads[clip_flat, side_index * per_side:(side_index + 1) * per_side] * inside.astype(jnp.float32)
            summed = summed.at[send_slots[s_index, t_index, side_index]].add(import_rows)
        owner_mask = active[s_index, t_index].astype(jnp.float32)[:, None, None, None]
        return (summed * owner_mask).astype(jnp.bfloat16)
    input_grad = lax.map(owner_grad, jnp.arange(device_count, dtype=jnp.int32))
    input_grad = input_grad.reshape(features.shape)
    output = outputs.reshape(features.shape)

    def band_map(weight_wide):
        return band_weights(weight_wide, channels)
    unused, pull_weight = jax.vjp(band_map, jnp.zeros(weight.shape, jnp.float32))
    weight_sum = pull_weight(band_grad)[0]
    grad_scale = float(device_count * slot_count * 512) ** (-0.5)
    bias_total = lax.optimization_barrier(jnp.sum(bias_sum.reshape(8, channels), axis=0))
    return (output, input_grad, weight_sum * grad_scale, bias_total * grad_scale)
```

```python
import jax
import jax.numpy as jnp
from jax import lax
from jax.experimental import pallas as pl
from jax.experimental.pallas import tpu as pltpu
from jax.sharding import PartitionSpec as P

F32 = jnp.float32
BF16 = jnp.bfloat16
DEVICE_SIDES = [(s, t) for s in (-1, 0, 1) for t in (-1, 0, 1) if (s, t) != (0, 0)]
SHELL = (
    [(0, y) for y in range(8)]
    + [(7, y) for y in range(8)]
    + [(x, 0) for x in range(1, 7)]
    + [(x, 7) for x in range(1, 7)]
)
ROWS = len(SHELL) + 9
VMEM = pl.BlockSpec(memory_space=pltpu.VMEM)
SMEM = pl.BlockSpec(memory_space=pltpu.SMEM)
PARAMS = pltpu.CompilerParams(vmem_limit_bytes=56 * 1024 * 1024)


def dot(a, b):
    return jnp.dot(a, b, preferred_element_type=F32)


def dot_nt(a, b):
    return lax.dot_general(a, b, (((1,), (1,)), ((), ())), preferred_element_type=F32)


def dot_tn(a, b):
    return lax.dot_general(a, b, (((0,), (0,)), ((), ())), preferred_element_type=F32)


def roll(v, by):
    by = by % 128
    return v if by == 0 else pltpu.roll(v, by, axis=1)


def lanes(n, width=128):
    return lax.broadcasted_iota(jnp.int32, (n, width), 1)


def one_hot(test):
    return jnp.where(test, 1.0, 0.0).astype(BF16)


def halves(h):
    return slice(128 * h, 128 * h + 128)


def pack_z(load, top, n, ys=range(8)):
    sub = lanes(n) // 32
    out = []
    for h in (0, 1):
        acc = None
        for k in range(4):
            y = 4 * h + k
            if y not in ys:
                continue
            v = load(y, halves(1 if top else 0)).astype(F32)
            v = roll(v, 32 * k - (96 if top else 0))
            acc = v if acc is None else jnp.where(sub == k, v, acc)
        out.append(acc)
    return out


def unpack_z(low, high, y, n):
    k = y % 4
    lane = lanes(n)
    zero = jnp.zeros((n, 128), F32)
    first = jnp.where(lane < 32, roll(low(halves(y // 4)), -32 * k), zero)
    second = jnp.where(lane >= 96, roll(high(halves(y // 4)), 96 - 32 * k), zero)
    return first, second


def squeeze(piece, g, k, h, n):
    lane = lanes(n)
    last = piece(4 * g + 3, h)
    if h == 0:
        return jnp.where(lane < 32, roll(last, -32 * (k + 1)), piece(4 * g + k, h))
    return jnp.where(lane >= 96, roll(last, 96 - 32 * k), piece(4 * g + k, h))


def unsqueeze(row, p, h, n):
    g, k = p // 4, p % 4
    if k < 3:
        return row(3 * g + k, h)
    sub = lanes(n) // 32
    acc = None
    for j in range(3):
        v = roll(row(3 * g + j, h), 32 * (j + 1) if h == 0 else 32 * j - 96)
        acc = v if acc is None else jnp.where(sub == (j + 1 if h == 0 else j), v, acc)
    return acc


def pack_kernel(count_ref, f_ref, slots_ref, fm_ref, *refs):
    outs, zp = refs[:8], refs[8]
    count = count_ref[0, 0]
    live = (lax.broadcasted_iota(jnp.int32, (64, 256), 0) < count).astype(F32)

    def mask_rows(r, _):
        fm_ref[r] = (f_ref[r].astype(F32) * live).astype(BF16)
        return _

    lax.fori_loop(0, 64, mask_rows, 0)
    chosen = one_hot(slots_ref[...] == lax.broadcasted_iota(jnp.int32, (128, 64), 1))

    def send(row, value):
        value = value.astype(BF16)
        for d in range(8):
            outs[d][row] = value[16 * d : 16 * d + 16]

    for row, (x, y) in enumerate(SHELL):
        send(row, dot(chosen, fm_ref[8 * x + y]))
    for x in range(1, 7):
        for s in (0, 1):
            h0, h1 = pack_z(lambda y, h: fm_ref[8 * x + y, :, h], s == 0, 64, range(1, 7))
            z = jnp.concatenate([h0, h1], axis=1).astype(BF16)
            zp[2 * (x - 1) + s] = dot(chosen, z)
    for g in range(3):
        for k in range(3):
            parts = [
                squeeze(lambda p, hh: zp[p, :, halves(hh)], g, k, h, 128) for h in (0, 1)
            ]
            send(28 + 3 * g + k, jnp.concatenate(parts, axis=1))


def pack(count, f_rows, slots_col):
    return pl.pallas_call(
        pack_kernel,
        out_shape=[jax.ShapeDtypeStruct((64, 64, 256), BF16)]
        + [jax.ShapeDtypeStruct((ROWS, 16, 256), BF16)] * 8,
        in_specs=[SMEM, VMEM, VMEM],
        out_specs=[VMEM] * 9,
        scratch_shapes=[pltpu.VMEM((12, 128, 256), F32)],
        compiler_params=PARAMS,
        name="pack",
    )(count, f_rows, slots_col)


def build_bands(wt_ref, bm_ref, bym_ref, bye_ref):
    blk = lanes(32, 256) // 32
    zero = jnp.zeros((32, 256), F32)

    def banded(w0, w1, w2, i):
        row = jnp.where(blk == i - 1, w2, zero)
        row = jnp.where(blk == i, w1, row)
        return jnp.where(blk == i + 1, w0, row).astype(BF16)

    def one(aq, _):
        w0, w1, w2 = (wt_ref[3 * aq + r].astype(F32) for r in range(3))
        for i in range(8):
            bm_ref[aq, 32 * i : 32 * i + 32, :] = banded(w0, w1, w2, i)
        return _

    lax.fori_loop(0, 9, one, 0)

    def side(a, _):
        for s in (0, 1):
            w0, w1, w2 = (wt_ref[9 * a + 3 * q + 2 * s].astype(F32) for q in range(3))
            k = 2 * a + s
            for i in range(8):
                bym_ref[k, 32 * i : 32 * i + 32, :] = banded(w0, w1, w2, i)
            bye_ref[k] = jnp.zeros((256, 256), BF16)
            bye_ref[k, 0:32, :] = jnp.where(blk == 7, w2, zero).astype(BF16)
            bye_ref[k, 224:256, :] = jnp.where(blk == 0, w0, zero).astype(BF16)
        return _

    lax.fori_loop(0, 3, side, 0)


def high_low(v):
    high = v.astype(BF16)
    return high, (v - high.astype(F32)).astype(BF16)


def dgrad_kernel(
    count_ref, g_ref, wt_ref, rows3_ref, rows2_ref,
    own_ref, gm_ref, gz_ref, bm_ref, bym_ref, bye_ref, *refs
):
    outs = refs[:8]
    gpad, gzpad, pg, ag, agx, xf, yf, tz, oht3, oht2 = refs[8:]
    count = count_ref[0, 0]
    build_bands(wt_ref, bm_ref, bym_ref, bye_ref)
    live = (lax.broadcasted_iota(jnp.int32, (64, 256), 0) < count).astype(F32)
    for i in (0, 1, 10, 11):
        gpad[i] = jnp.zeros((8, 64, 256), BF16)
        gzpad[0, i] = jnp.zeros((64, 256), BF16)
        gzpad[1, i] = jnp.zeros((64, 256), BF16)
    pg[:, 0] = jnp.zeros((10, 64, 256), F32)
    pg[:, 9] = jnp.zeros((10, 64, 256), F32)

    def load_g(x, _):
        for y in range(8):
            v = (g_ref[8 * x + y].astype(F32) * live).astype(BF16)
            gpad[x + 2, y] = v
            gm_ref[8 * x + y] = v
        for s in (0, 1):
            parts = pack_z(lambda y, h: gpad[x + 2, y, :, h], s == 1, 64)
            z = jnp.concatenate(parts, axis=1).astype(BF16)
            gzpad[s, x + 2] = z
            gz_ref[s, x] = z
        return _

    lax.fori_loop(0, 8, load_g, 0)
    tsub = lax.broadcasted_iota(jnp.int32, (192, 192), 0)
    tsub2 = lax.broadcasted_iota(jnp.int32, (192, 128), 0)
    for k in range(9):
        oht3[k] = one_hot(rows3_ref[k : k + 1, :] == tsub)
        oht2[k] = one_hot(rows2_ref[k : k + 1, :] == tsub2)

    def plane(u, _):
        for q in (1, 0, 2):
            acc = None
            for a in range(3):
                part = dot_nt(gpad[u + 2 - a].reshape(512, 256), bm_ref[3 * a + q])
                acc = part if acc is None else acc + part
            acc = acc.reshape(8, 64, 256)
            if q == 1:
                pg[u, 1:9] = acc
            elif q == 0:
                pg[u, 0:8] = pg[u, 0:8] + acc
            else:
                pg[u, 2:10] = pg[u, 2:10] + acc
        return _

    lax.fori_loop(0, 10, plane, 0)
    for s in (0, 1):
        main, extra = None, None
        for a in range(3):
            z = gzpad[s, 2 - a : 12 - a].reshape(640, 256)
            pm = dot_nt(z, bym_ref[2 * a + s])
            pe = dot_nt(z, bye_ref[2 * a + s])
            main = pm if main is None else main + pm
            extra = pe if extra is None else extra + pe
        ag[s] = main.reshape(10, 64, 256)
        agx[s] = extra.reshape(10, 64, 256)

    def spread(k, v):
        high, low = high_low(v)
        return dot(oht2[k], jnp.concatenate([high, low], axis=0))

    lane = lanes(64, 256)

    def spread_z(k, s, u):
        m, e = ag[s, u], agx[s, u]
        zero = jnp.zeros_like(e)
        v = jnp.concatenate(
            [jnp.where(lane >= 224, e, zero), m, jnp.where(lane < 32, e, zero)], axis=0
        )
        high, low = high_low(v)
        return dot(oht3[k], high) + dot(oht3[k], low)

    def inner(x, _):
        yf[0, x] = spread(3, pg[x + 1, 0])
        yf[1, x] = spread(5, pg[x + 1, 9])
        for s in (0, 1):
            tz[s, x] = spread_z(3 + 2 * s, s, x + 1)
        return _

    lax.fori_loop(0, 8, inner, 0)
    for i, (u, x, ex) in enumerate(((0, 7, 0), (9, 0, 2))):
        def along(y, _, i=i, u=u, ex=ex):
            xf[i, y] = spread(3 * ex + 1, pg[u, y + 1])
            return _

        lax.fori_loop(0, 8, along, 0)
        yf[0, x] = yf[0, x] + spread(3 * ex, pg[u, 0])
        yf[1, x] = yf[1, x] + spread(3 * ex + 2, pg[u, 9])
        for s in (0, 1):
            tz[s, x] = tz[s, x] + spread_z(3 * ex + 2 * s, s, u)

    def own(x, _):
        for y in range(8):
            first, second = unpack_z(
                lambda h: tz[1, x, 0:64, h], lambda h: tz[0, x, 0:64, h], y, 64
            )
            extra = jnp.concatenate([first, second], axis=1)
            v = pg[x + 1, y + 1] + extra
            if y == 7:
                v = v + yf[0, x, 0:64, :]
            if y == 0:
                v = v + yf[1, x, 0:64, :]
            own_ref[8 * x + y] = v
        return _

    lax.fori_loop(0, 8, own, 0)
    for i, x in enumerate((7, 0)):
        for y in range(8):
            own_ref[8 * x + y] = own_ref[8 * x + y] + xf[i, y, 0:64, :]

    def give(row, value):
        value = value.astype(BF16)
        for d in range(8):
            outs[d][row] = value[16 * d : 16 * d + 16]

    far = slice(64, 192)
    for row, (x, y) in enumerate(SHELL):
        first, second = unpack_z(lambda h: tz[1, x, far, h], lambda h: tz[0, x, far, h], y, 128)
        v = jnp.concatenate([first, second], axis=1)
        if x in (0, 7):
            v = v + xf[0 if x == 7 else 1, y, far, :]
        if y in (0, 7):
            v = v + yf[0 if y == 7 else 1, x, far, :]
        give(row, v)
    for g in range(3):
        for k in range(3):
            parts = [
                squeeze(lambda p, hh: tz[p % 2, 1 + p // 2, far, halves(hh)], g, k, h, 128)
                for h in (0, 1)
            ]
            give(28 + 3 * g + k, jnp.concatenate(parts, axis=1))


def dgrad(count, g_rows, wt, rows3, rows2):
    sd = jax.ShapeDtypeStruct
    return pl.pallas_call(
        dgrad_kernel,
        out_shape=[
            sd((64, 64, 256), F32),
            sd((64, 64, 256), BF16),
            sd((2, 8, 64, 256), BF16),
            sd((9, 256, 256), BF16),
            sd((6, 256, 256), BF16),
            sd((6, 256, 256), BF16),
        ]
        + [sd((ROWS, 16, 256), BF16)] * 8,
        in_specs=[SMEM] + [VMEM] * 4,
        out_specs=[VMEM] * 14,
        scratch_shapes=[
            pltpu.VMEM((12, 8, 64, 256), BF16),
            pltpu.VMEM((2, 12, 64, 256), BF16),
            pltpu.VMEM((10, 10, 64, 256), F32),
            pltpu.VMEM((2, 10, 64, 256), F32),
            pltpu.VMEM((2, 10, 64, 256), F32),
            pltpu.VMEM((2, 8, 192, 256), F32),
            pltpu.VMEM((2, 8, 192, 256), F32),
            pltpu.VMEM((2, 8, 192, 256), F32),
            pltpu.VMEM((9, 192, 192), BF16),
            pltpu.VMEM((9, 192, 128), BF16),
        ],
        compiler_params=PARAMS,
        name="dgrad",
    )(count, g_rows, wt, rows3, rows2)


def wgrad_kernel(fm_ref, gm_ref, gz_ref, cols_ref, *refs):
    ins = refs[:8]
    vm_ref, a_ref, ax_ref, dw_ref = refs[8:12]
    xt, yt, tz, oh3, acc, fold = refs[12:]
    far = slice(64, 192)
    tl = lanes(192, 192)
    for k in range(9):
        oh3[k] = one_hot(cols_ref[:, k : k + 1] == tl)
    for row, (x, y) in enumerate(SHELL):
        places = []
        if x in (0, 7):
            places.append((xt, 0 if x == 7 else 1, y))
        if y in (0, 7):
            places.append((yt, 0 if y == 7 else 1, x))
        for ref, i, j in places:
            ref[i, j, 0:64, :] = fm_ref[8 * x + y]
            for d in range(8):
                ref[i, j, 64 + 16 * d : 80 + 16 * d, :] = ins[d][row]

    def own_z(x, _):
        for s in (0, 1):
            parts = pack_z(lambda y, h: fm_ref[8 * x + y, :, h], s == 0, 64)
            tz[s, x, 0:64, :] = jnp.concatenate(parts, axis=1).astype(BF16)
        return _

    lax.fori_loop(0, 8, own_z, 0)
    for i, x in enumerate((7, 0)):
        for s in (0, 1):
            parts = pack_z(lambda y, h: xt[i, y, far, h], s == 0, 128)
            tz[s, x, far, :] = jnp.concatenate(parts, axis=1).astype(BF16)

    def compact(row, h):
        return jnp.concatenate([ins[d][28 + row, :, halves(h)] for d in range(8)], axis=0).astype(F32)

    sub = lanes(128) // 32
    for x in range(1, 7):
        for s in (0, 1):
            top = s == 0
            src = halves(1 if top else 0)
            first = unsqueeze(compact, 2 * (x - 1) + s, 0, 128)
            second = unsqueeze(compact, 2 * (x - 1) + s, 1, 128)
            y0 = roll(yt[1, x, far, src].astype(F32), -96 if top else 0)
            y7 = roll(yt[0, x, far, src].astype(F32), 96 - (96 if top else 0))
            first = jnp.where(sub == 0, y0, first)
            second = jnp.where(sub == 3, y7, second)
            tz[s, x, far, :] = jnp.concatenate([first, second], axis=1).astype(BF16)

    lane = lanes(64, 256)

    def halo_z(k, s, x, u):
        v = dot(oh3[k], tz[s, x])
        zero = jnp.zeros((64, 256), F32)
        a_ref[s, u] = v[64:128].astype(BF16)
        ax_ref[s, u] = jnp.where(
            lane >= 224, v[0:64], jnp.where(lane < 32, v[128:192], zero)
        ).astype(BF16)

    def fill(x, _):
        for y in range(8):
            vm_ref[x + 1, y + 1] = fm_ref[8 * x + y]
        vm_ref[x + 1, 0] = dot(oh3[4, 0:64, :], yt[0, x]).astype(BF16)
        vm_ref[x + 1, 9] = dot(oh3[4, 128:192, :], yt[1, x]).astype(BF16)
        for s in (0, 1):
            halo_z(3 + 2 * s, s, x, x + 1)
        return _

    lax.fori_loop(0, 8, fill, 0)
    for i, (u, x, ex) in enumerate(((0, 7, 0), (9, 0, 2))):
        def along(y, _, i=i, u=u, ex=ex):
            vm_ref[u, y + 1] = dot(oh3[3 * ex + 1, 64:128, :], xt[i, y]).astype(BF16)
            return _

        lax.fori_loop(0, 8, along, 0)
        vm_ref[u, 0] = dot(oh3[3 * ex + 1, 0:64, :], xt[i, 7]).astype(BF16)
        vm_ref[u, 9] = dot(oh3[3 * ex + 1, 128:192, :], xt[i, 0]).astype(BF16)
        for s in (0, 1):
            halo_z(3 * ex + 2 * s, s, x, u)

    def column(x, a, q):
        return vm_ref[x + a, q : q + 8].reshape(512, 256)

    def sums(x, bias):
        g = gm_ref[pl.ds(8 * x, 8)].reshape(512, 256)
        cols = jnp.concatenate([column(x, a, q) for a in range(3) for q in range(3)], axis=1)
        part = dot_tn(g, cols)

        @pl.when(x == 0)
        def _():
            acc[:, 0:2304] = part

        @pl.when(x != 0)
        def _():
            acc[:, 0:2304] = acc[:, 0:2304] + part

        return bias + jnp.sum(g.astype(F32).reshape(64, 8, 256), axis=0)

    bias = lax.fori_loop(0, 8, sums, jnp.zeros((8, 256), F32))
    for s in (0, 1):
        z = gz_ref[s].reshape(512, 256)
        cols = jnp.concatenate(
            [r[s, a : a + 8].reshape(512, 256) for a in range(3) for r in (a_ref, ax_ref)], axis=1
        )
        acc[:, 2304 + 1536 * s : 3840 + 1536 * s] = dot_tn(z, cols)

    blk = lanes(32, 256) // 32

    def band_sum(start, r):
        total = None
        for i in range(8):
            if not 0 <= i + r - 1 < 8:
                continue
            v = acc[32 * i : 32 * i + 32, start : start + 256]
            v = jnp.where(blk == i + r - 1, v, jnp.zeros_like(v))
            total = v if total is None else total + v
        return total

    def fold_lanes(total):
        v = total[:, 0:128] + total[:, 128:256]
        v = v + pltpu.roll(v, 64, axis=1)
        return v + pltpu.roll(v, 32, axis=1)

    for a in range(3):
        for q in range(3):
            for r in range(3):
                total = band_sum(256 * (3 * a + q), r)
                if r != 1:
                    s = r // 2
                    base = 2304 + 1536 * s + 512 * a
                    total = total + band_sum(base, q)
                    if q == 0:
                        v = acc[0:32, base + 256 : base + 512]
                        total = total + jnp.where(blk == 7, v, jnp.zeros_like(v))
                    if q == 2:
                        v = acc[224:256, base + 256 : base + 512]
                        total = total + jnp.where(blk == 0, v, jnp.zeros_like(v))
                t = 9 * a + 3 * q + r
                fold[32 * t : 32 * t + 32, :] = fold_lanes(total)
    quarter = lanes(216) // 32
    v = fold[0:216, :]
    for k in range(1, 4):
        v = jnp.where(quarter == k, fold[216 * k : 216 * k + 216, :], v)
    dw_ref[0:216, :] = v
    dw_ref[216:224, :] = fold_lanes(bias)


def wgrad(fm, gm, gz, cols3, arrived):
    sd = jax.ShapeDtypeStruct
    return pl.pallas_call(
        wgrad_kernel,
        out_shape=[
            sd((10, 10, 64, 256), BF16),
            sd((2, 10, 64, 256), BF16),
            sd((2, 10, 64, 256), BF16),
            sd((224, 128), F32),
        ],
        in_specs=[VMEM] * 12,
        out_specs=[VMEM] * 4,
        scratch_shapes=[
            pltpu.VMEM((2, 8, 192, 256), BF16),
            pltpu.VMEM((2, 8, 192, 256), BF16),
            pltpu.VMEM((2, 8, 192, 256), BF16),
            pltpu.VMEM((9, 192, 192), BF16),
            pltpu.VMEM((256, 5376), F32),
            pltpu.VMEM((864, 128), F32),
        ],
        compiler_params=PARAMS,
        name="wgrad",
    )(fm, gm, gz, cols3, *arrived)


def forward_kernel(count_ref, vm_ref, a_ref, ax_ref, bm_ref, bym_ref, bye_ref, bias_ref, out_ref, es):
    count = count_ref[0, 0]
    live = (lax.broadcasted_iota(jnp.int32, (64, 256), 0) < count).astype(F32)
    for s in (0, 1):
        total = None
        for a in range(3):
            for ref, band in ((a_ref, bym_ref), (ax_ref, bye_ref)):
                part = dot(ref[s, a : a + 8].reshape(512, 256), band[2 * a + s])
                total = part if total is None else total + part
        es[s] = total.reshape(8, 64, 256)
    bias = bias_ref[...]

    def plane(x, _):
        cols = jnp.concatenate(
            [vm_ref[x + a, q : q + 8].reshape(512, 256) for a in range(3) for q in range(3)], axis=1
        )
        total = dot(cols, bm_ref[...].reshape(2304, 256)).reshape(8, 64, 256)
        for y in range(8):
            first, second = unpack_z(lambda h: es[0, x, :, h], lambda h: es[1, x, :, h], y, 64)
            v = total[y] + jnp.concatenate([first, second], axis=1) + bias
            out_ref[8 * x + y] = (v * live).astype(BF16)
        return _

    lax.fori_loop(0, 8, plane, 0)


def forward(count, vm, a, ax, bm, bym, bye, bias_row):
    return pl.pallas_call(
        forward_kernel,
        out_shape=jax.ShapeDtypeStruct((64, 64, 256), BF16),
        in_specs=[SMEM] + [VMEM] * 7,
        out_specs=VMEM,
        scratch_shapes=[pltpu.VMEM((2, 8, 64, 256), F32)],
        compiler_params=PARAMS,
        name="forward",
    )(count, vm, a, ax, bm, bym, bye, bias_row)


def finish_kernel(count_ref, own_ref, slots_ref, *refs):
    ins, out_ref, zp = refs[:8], refs[8], refs[9]
    count = count_ref[0, 0]
    live = (lax.broadcasted_iota(jnp.int32, (64, 256), 0) < count).astype(F32)
    chosen = one_hot(slots_ref[...] == lax.broadcasted_iota(jnp.int32, (64, 128), 0))

    def back(row):
        return dot(chosen, jnp.concatenate([r[row] for r in ins], axis=0))

    for row, (x, y) in enumerate(SHELL):
        v = own_ref[8 * x + y] + back(row)
        out_ref[8 * x + y] = (v * live).astype(BF16)
    for k in range(9):
        zp[k] = back(28 + k)

    def piece(x, s, h):
        return unsqueeze(lambda row, hh: zp[row, :, halves(hh)], 2 * (x - 1) + s, h, 64)

    for x in range(1, 7):
        parts = {(s, h): piece(x, s, h) for s in (0, 1) for h in (0, 1)}
        for y in range(1, 7):
            first, second = unpack_z(
                lambda h: parts[1, h.start // 128], lambda h: parts[0, h.start // 128], y, 64
            )
            v = own_ref[8 * x + y] + jnp.concatenate([first, second], axis=1)
            out_ref[8 * x + y] = (v * live).astype(BF16)


def finish(count, own, slots_row, returned):
    return pl.pallas_call(
        finish_kernel,
        out_shape=jax.ShapeDtypeStruct((64, 64, 256), BF16),
        in_specs=[SMEM] + [VMEM] * 10,
        out_specs=VMEM,
        scratch_shapes=[pltpu.VMEM((9, 64, 256), F32)],
        compiler_params=PARAMS,
        name="finish",
    )(count, own, slots_row, *returned)


def side_pairs(ds, dt):
    spaces, tiles = lax.axis_size("space"), lax.axis_size("tile")
    return [
        (s * tiles + t, (s + ds) * tiles + t + dt)
        for s in range(spaces)
        for t in range(tiles)
        if 0 <= s + ds < spaces and 0 <= t + dt < tiles
    ]


def send_out(blocks):
    return [
        lax.ppermute(b, ("space", "tile"), side_pairs(ds, dt))
        for b, (ds, dt) in zip(blocks, DEVICE_SIDES)
    ]


def send_back(blocks):
    return [
        lax.ppermute(b, ("space", "tile"), side_pairs(-ds, -dt))
        for b, (ds, dt) in zip(blocks, DEVICE_SIDES)
    ]


def sum_all(value):
    for axis in ("tile", "space"):
        n = lax.axis_size(axis)
        if n & (n - 1):
            value = lax.psum(value, axis)
            continue
        by = 1
        while by < n:
            value = value + lax.ppermute(value, axis, [(i, i ^ by) for i in range(n)])
            by *= 2
    return value


def to_rows(v):
    return jnp.transpose(v[0, 0].reshape(64, 64, 256), (1, 0, 2))


def from_rows(v):
    return jnp.transpose(v, (1, 0, 2)).reshape(1, 1, 64, 8, 8, 256)


def local(features, weight, bias_vector, cotangent, counts, send_slots, neighbours):
    slots = send_slots[0, 0].reshape(1, 128)
    near = neighbours[0, 0]
    full = jnp.concatenate(
        [near[:, :13], jnp.full((64, 1), 192, jnp.int32), near[:, 13:]], axis=1
    ).reshape(64, 3, 3, 3)
    cols3 = jnp.transpose(full, (2, 0, 1, 3)).reshape(192, 9)
    rows3 = cols3.T
    rows2 = full[:, :, :, 1].reshape(64, 9).T
    rows2 = jnp.concatenate([rows2, rows2], axis=1)
    wt = jnp.tile(weight.reshape(27, 32, 32), (1, 1, 8))
    bias_row = jnp.tile(bias_vector, 8).reshape(1, 256)

    fm, *outgoing = pack(counts, to_rows(features), slots.reshape(128, 1))
    arrived = send_out(outgoing)
    own, gm, gz, bm, bym, bye, *back = dgrad(counts, to_rows(cotangent), wt, rows3, rows2)
    returned = send_back(back)
    vm, a, ax, dw = wgrad(fm, gm, gz, cols3, arrived)
    out = forward(counts, vm, a, ax, bm, bym, bye, bias_row)
    total = sum_all(dw)
    grad_in = finish(counts, own, slots, returned)

    scale = float(lax.axis_size("space") * lax.axis_size("tile") * 64 * 512) ** (-0.5)
    total = total * scale
    weight_grad = jnp.transpose(total[:216].reshape(216, 4, 32), (1, 0, 2)).reshape(27, 32, 32)
    weight_grad = jnp.transpose(weight_grad, (0, 2, 1)).reshape(3, 3, 3, 32, 32)
    bias_grad = jnp.sum(total[216:224, :32], axis=0)
    return from_rows(out), from_rows(grad_in), weight_grad, bias_grad


def solution(mesh):
    wide = P("space", "tile", None, None, None, None)
    return jax.shard_map(
        local,
        mesh=mesh,
        in_specs=(wide, P(), P(), wide, P("space", "tile"), P("space", "tile", None, None), P("space", "tile", None, None)),
        out_specs=(wide, wide, P(), P()),
        check_vma=False,
    )
```

```python
import functools

import jax
import jax.numpy as jnp
from jax import lax
from jax.experimental import pallas as pl
from jax.experimental.pallas import tpu as pltpu
from jax.sharding import PartitionSpec as P

F32 = jnp.float32
BF16 = jnp.bfloat16
DEVICE_SIDES = [(s, t) for s in (-1, 0, 1) for t in (-1, 0, 1) if (s, t) != (0, 0)]
SHELL = (
    [(0, y) for y in range(8)]
    + [(7, y) for y in range(8)]
    + [(x, 0) for x in range(1, 7)]
    + [(x, 7) for x in range(1, 7)]
)
ROWS = len(SHELL) + 9
UNROLL = 8
XS = 4
VMEM = pl.BlockSpec(memory_space=pltpu.VMEM)
SMEM = pl.BlockSpec(memory_space=pltpu.SMEM)
ANY = pl.BlockSpec(memory_space=pl.ANY)
DMA = pltpu.SemaphoreType.DMA
PARAMS = pltpu.CompilerParams(vmem_limit_bytes=56 * 1024 * 1024)


def cost(us):
    return pl.CostEstimate(flops=us * 10**6, bytes_accessed=us * 10**3, transcendentals=0)


def dot(a, b):
    return jnp.dot(a, b, preferred_element_type=F32)


def dot_nt(a, b):
    return lax.dot_general(a, b, (((1,), (1,)), ((), ())), preferred_element_type=F32)


def dot_tn(a, b):
    return lax.dot_general(a, b, (((0,), (0,)), ((), ())), preferred_element_type=F32)


def roll(v, by):
    by = by % 128
    return v if by == 0 else pltpu.roll(v, by, axis=1)


def lanes(n, width=128):
    return lax.broadcasted_iota(jnp.int32, (n, width), 1)


def one_hot(test):
    return jnp.where(test, 1.0, 0.0).astype(BF16)


def halves(h):
    return slice(128 * h, 128 * h + 128)


def pack_z(load, top, n, ys=range(8)):
    sub = lanes(n) // 32
    out = []
    for h in (0, 1):
        acc = None
        for k in range(4):
            y = 4 * h + k
            if y not in ys:
                continue
            v = load(y, halves(1 if top else 0)).astype(F32)
            v = roll(v, 32 * k - (96 if top else 0))
            acc = v if acc is None else jnp.where(sub == k, v, acc)
        out.append(acc)
    return out


def unpack_z(low, high, y, n):
    k = y % 4
    lane = lanes(n)
    zero = jnp.zeros((n, 128), F32)
    first = jnp.where(lane < 32, roll(low(halves(y // 4)), -32 * k), zero)
    second = jnp.where(lane >= 96, roll(high(halves(y // 4)), 96 - 32 * k), zero)
    return first, second


def squeeze(piece, g, k, h, n):
    lane = lanes(n)
    last = piece(4 * g + 3, h)
    if h == 0:
        return jnp.where(lane < 32, roll(last, -32 * (k + 1)), piece(4 * g + k, h))
    return jnp.where(lane >= 96, roll(last, 96 - 32 * k), piece(4 * g + k, h))


def unsqueeze(row, p, h, n):
    g, k = p // 4, p % 4
    if k < 3:
        return row(3 * g + k, h)
    sub = lanes(n) // 32
    acc = None
    for j in range(3):
        v = roll(row(3 * g + j, h), 32 * (j + 1) if h == 0 else 32 * j - 96)
        acc = v if acc is None else jnp.where(sub == (j + 1 if h == 0 else j), v, acc)
    return acc


def pack_kernel(count_ref, f_ref, slots_ref, fm_ref, right, left, down, up, zp):
    count = count_ref[0, 0]
    live = (lax.broadcasted_iota(jnp.int32, (64, 256), 0) < count).astype(F32)

    def mask_rows(i, _):
        rows = pl.ds(16 * i, 16)
        v = jnp.transpose(f_ref[:, rows, :], (1, 0, 2))
        fm_ref[rows] = v * live[None].astype(BF16)
        return _

    lax.fori_loop(0, 4, mask_rows, 0)
    chosen = one_hot(slots_ref[...] == lax.broadcasted_iota(jnp.int32, (128, 64), 1))

    def send(row, value):
        value = value.astype(BF16)
        for ref, order in ((right, (4, 7, 2)), (left, (3, 5, 0)), (down, (1,)), (up, (6,))):
            for i, d in enumerate(order):
                ref[row, 16 * i : 16 * i + 16, :] = value[16 * d : 16 * d + 16]

    for row, (x, y) in enumerate(SHELL):
        send(row, dot(chosen, fm_ref[8 * x + y]))
    for x in range(1, 7):
        for s in (0, 1):
            h0, h1 = pack_z(lambda y, h: fm_ref[8 * x + y, :, h], s == 0, 64, range(1, 7))
            z = jnp.concatenate([h0, h1], axis=1).astype(BF16)
            zp[2 * (x - 1) + s] = dot(chosen, z)
    for g in range(3):
        for k in range(3):
            parts = [
                squeeze(lambda p, hh: zp[p, :, halves(hh)], g, k, h, 128) for h in (0, 1)
            ]
            send(28 + 3 * g + k, jnp.concatenate(parts, axis=1))


def pack(count, f_rows, slots_col):
    return pl.pallas_call(
        pack_kernel,
        out_shape=[jax.ShapeDtypeStruct((64, 64, 256), BF16)]
        + [jax.ShapeDtypeStruct((ROWS, n, 256), BF16) for n in (48, 48, 16, 16)],
        in_specs=[SMEM, VMEM, VMEM],
        out_specs=[VMEM] * 5,
        scratch_shapes=[pltpu.VMEM((12, 128, 256), F32)],
        compiler_params=PARAMS,
        cost_estimate=cost(5),
        name="pack",
    )(count, f_rows, slots_col)


def build_bands(wt_ref, bm_ref, bym_ref, bye_ref):
    blk = lanes(32, 256) // 32
    zero = jnp.zeros((32, 256), F32)

    def banded(w0, w1, w2, i):
        row = jnp.where(blk == i - 1, w2, zero)
        row = jnp.where(blk == i, w1, row)
        return jnp.where(blk == i + 1, w0, row).astype(BF16)

    def one(aq, _):
        w0, w1, w2 = (wt_ref[3 * aq + r].astype(F32) for r in range(3))
        for i in range(8):
            bm_ref[aq, 32 * i : 32 * i + 32, :] = banded(w0, w1, w2, i)
        return _

    lax.fori_loop(0, 9, one, 0)

    def side(a, _):
        for s in (0, 1):
            w0, w1, w2 = (wt_ref[9 * a + 3 * q + 2 * s].astype(F32) for q in range(3))
            k = 2 * a + s
            for i in range(8):
                bym_ref[k, 32 * i : 32 * i + 32, :] = banded(w0, w1, w2, i)
            bye_ref[k] = jnp.zeros((256, 256), BF16)
            bye_ref[k, 0:32, :] = jnp.where(blk == 7, w2, zero).astype(BF16)
            bye_ref[k, 224:256, :] = jnp.where(blk == 0, w0, zero).astype(BF16)
        return _

    lax.fori_loop(0, 3, side, 0)


def high_low(v):
    high = v.astype(BF16)
    return high, (v - high.astype(F32)).astype(BF16)


def dgrad_kernel(
    count_ref, g_ref, wt_ref, rows3_ref, rows2_ref,
    own_hbm, gm_hbm, gz_hbm, bm_hbm, bym_hbm, bye_hbm, bias_ref, *refs
):
    to_left, to_right, below, above = refs[:4]
    own_ref, bm_ref, bym_ref, bye_ref, gt, gzt, gpad, gzpad, pg, ag, agx, xf, yf, tz, oht3, oht2, sems = refs[4:]
    count = count_ref[0, 0]
    build_bands(wt_ref, bm_ref, bym_ref, bye_ref)
    stores = [
        pltpu.make_async_copy(src, dst, sems.at[i])
        for i, (src, dst) in enumerate(
            (
                (bm_ref, bm_hbm),
                (bym_ref, bym_hbm),
                (bye_ref, bye_hbm),
                (gt, gm_hbm),
                (gzt, gz_hbm),
                (own_ref, own_hbm),
            )
        )
    ]
    for c in stores[:3]:
        c.start()
    live = (lax.broadcasted_iota(jnp.int32, (64, 256), 0) < count).astype(F32)
    for i in (0, 1, 10, 11):
        gpad[i] = jnp.zeros((8, 64, 256), BF16)
        gzpad[0, i] = jnp.zeros((64, 256), BF16)
        gzpad[1, i] = jnp.zeros((64, 256), BF16)
    pg[:, 0] = jnp.zeros((10, 64, 256), F32)
    pg[:, 9] = jnp.zeros((10, 64, 256), F32)

    def load_g(x, _):
        both = jnp.transpose(g_ref[:, pl.ds(16 * x, 16), :], (1, 0, 2)) * live[None].astype(BF16)
        gpad[pl.ds(2 * x + 2, 2)] = both.reshape(2, 8, 64, 256)
        for i in (0, 1):
            for s in (0, 1):
                parts = pack_z(lambda y, h: gpad[2 * x + i + 2, y, :, h], s == 1, 64)
                z = jnp.concatenate(parts, axis=1).astype(BF16)
                gzpad[s, 2 * x + i + 2] = z
        return _

    lax.fori_loop(0, 4, load_g, 0)
    bias = jnp.zeros((8, 256), F32)
    for x in range(8):
        g = gpad[x + 2].reshape(512, 256)
        gt[:, 512 * x : 512 * x + 512] = g.T
        bias = bias + jnp.sum(g.astype(F32).reshape(64, 8, 256), axis=0)
    bias_ref[...] = bias
    for s in (0, 1):
        gzt[s] = gzpad[s, 2:10].reshape(512, 256).T
    for c in stores[3:5]:
        c.start()
    tsub = lax.broadcasted_iota(jnp.int32, (192, 192), 0)
    tsub2 = lax.broadcasted_iota(jnp.int32, (192, 128), 0)
    for k in range(9):
        oht3[k] = one_hot(rows3_ref[k : k + 1, :] == tsub)
        oht2[k] = one_hot(rows2_ref[k : k + 1, :] == tsub2)

    def plane(u, _):
        for q in (1, 0, 2):
            acc = None
            for a in range(3):
                part = dot_nt(gpad[u + 2 - a].reshape(512, 256), bm_ref[3 * a + q])
                acc = part if acc is None else acc + part
            acc = acc.reshape(8, 64, 256)
            if q == 1:
                pg[u, 1:9] = acc
            elif q == 0:
                pg[u, 0:8] = pg[u, 0:8] + acc
            else:
                pg[u, 2:10] = pg[u, 2:10] + acc
        return _

    lax.fori_loop(0, 10, plane, 0)
    for s in (0, 1):
        main, extra = None, None
        for a in range(3):
            z = gzpad[s, 2 - a : 12 - a].reshape(640, 256)
            pm = dot_nt(z, bym_ref[2 * a + s])
            pe = dot_nt(z, bye_ref[2 * a + s])
            main = pm if main is None else main + pm
            extra = pe if extra is None else extra + pe
        ag[s] = main.reshape(10, 64, 256)
        agx[s] = extra.reshape(10, 64, 256)

    def spread(k, v):
        high, low = high_low(v)
        return dot(oht2[k], jnp.concatenate([high, low], axis=0))

    lane = lanes(64, 256)

    def spread_z(k, s, u):
        m, e = ag[s, u], agx[s, u]
        zero = jnp.zeros_like(e)
        v = jnp.concatenate(
            [jnp.where(lane >= 224, e, zero), m, jnp.where(lane < 32, e, zero)], axis=0
        )
        high, low = high_low(v)
        return dot(oht3[k], high) + dot(oht3[k], low)

    def inner(x, _):
        yf[0, x] = spread(3, pg[x + 1, 0])
        yf[1, x] = spread(5, pg[x + 1, 9])
        for s in (0, 1):
            tz[s, x] = spread_z(3 + 2 * s, s, x + 1)
        return _

    lax.fori_loop(0, 8, inner, 0, unroll=UNROLL)
    for i, (u, x, ex) in enumerate(((0, 7, 0), (9, 0, 2))):
        def along(y, _, i=i, u=u, ex=ex):
            xf[i, y] = spread(3 * ex + 1, pg[u, y + 1])
            return _

        lax.fori_loop(0, 8, along, 0, unroll=UNROLL)
        yf[0, x] = yf[0, x] + spread(3 * ex, pg[u, 0])
        yf[1, x] = yf[1, x] + spread(3 * ex + 2, pg[u, 9])
        for s in (0, 1):
            tz[s, x] = tz[s, x] + spread_z(3 * ex + 2 * s, s, u)

    def own(x, _):
        for y in range(8):
            first, second = unpack_z(
                lambda h: tz[1, x, 0:64, h], lambda h: tz[0, x, 0:64, h], y, 64
            )
            extra = jnp.concatenate([first, second], axis=1)
            v = pg[x + 1, y + 1] + extra
            if y == 7:
                v = v + yf[0, x, 0:64, :]
            if y == 0:
                v = v + yf[1, x, 0:64, :]
            own_ref[8 * x + y] = v
        return _

    lax.fori_loop(0, 8, own, 0)
    for i, x in enumerate((7, 0)):
        for y in range(8):
            own_ref[8 * x + y] = own_ref[8 * x + y] + xf[i, y, 0:64, :]

    stores[5].start()

    def give(row, value):
        value = value.astype(BF16)
        for ref, order in ((to_left, (4, 7, 2)), (to_right, (3, 5, 0)), (below, (6,)), (above, (1,))):
            for i, d in enumerate(order):
                ref[row, 16 * i : 16 * i + 16, :] = value[16 * d : 16 * d + 16]

    far = slice(64, 192)
    for row, (x, y) in enumerate(SHELL):
        first, second = unpack_z(lambda h: tz[1, x, far, h], lambda h: tz[0, x, far, h], y, 128)
        v = jnp.concatenate([first, second], axis=1)
        if x in (0, 7):
            v = v + xf[0 if x == 7 else 1, y, far, :]
        if y in (0, 7):
            v = v + yf[0 if y == 7 else 1, x, far, :]
        give(row, v)
    for g in range(3):
        for k in range(3):
            parts = [
                squeeze(lambda p, hh: tz[p % 2, 1 + p // 2, far, halves(hh)], g, k, h, 128)
                for h in (0, 1)
            ]
            give(28 + 3 * g + k, jnp.concatenate(parts, axis=1))
    for c in stores:
        c.wait()


def dgrad(count, g_rows, wt, rows3, rows2):
    sd = jax.ShapeDtypeStruct
    return pl.pallas_call(
        dgrad_kernel,
        out_shape=[
            sd((64, 64, 256), F32),
            sd((256, 4096), BF16),
            sd((2, 256, 512), BF16),
            sd((9, 256, 256), BF16),
            sd((6, 256, 256), BF16),
            sd((6, 256, 256), BF16),
            sd((8, 256), F32),
        ]
        + [sd((ROWS, n, 256), BF16) for n in (48, 48, 16, 16)],
        in_specs=[SMEM] + [VMEM] * 4,
        out_specs=[ANY] * 6 + [VMEM] * 5,
        scratch_shapes=[
            pltpu.VMEM((64, 64, 256), F32),
            pltpu.VMEM((9, 256, 256), BF16),
            pltpu.VMEM((6, 256, 256), BF16),
            pltpu.VMEM((6, 256, 256), BF16),
            pltpu.VMEM((256, 4096), BF16),
            pltpu.VMEM((2, 256, 512), BF16),
            pltpu.VMEM((12, 8, 64, 256), BF16),
            pltpu.VMEM((2, 12, 64, 256), BF16),
            pltpu.VMEM((10, 10, 64, 256), F32),
            pltpu.VMEM((2, 10, 64, 256), F32),
            pltpu.VMEM((2, 10, 64, 256), F32),
            pltpu.VMEM((2, 8, 192, 256), F32),
            pltpu.VMEM((2, 8, 192, 256), F32),
            pltpu.VMEM((2, 8, 192, 256), F32),
            pltpu.VMEM((9, 192, 192), BF16),
            pltpu.VMEM((9, 192, 128), BF16),
            DMA((6,)),
        ],
        compiler_params=PARAMS,
        cost_estimate=cost(20000),
        name="dgrad",
    )(count, g_rows, wt, rows3, rows2)


def wgrad_kernel(fm_hbm, gm_hbm, gz_hbm, cols_ref, bias_ref, mark_hbm, *refs):
    far_hbm, (vm_hbm, a_hbm, ax_hbm, dw_ref) = refs[:4], refs[4:8]
    fm_ref, gm_ref, gz_ref, vm_ref, a_ref, ax_ref = refs[8:14]
    fars, (xt, yt, tz, oh3, acc, fold, sems) = refs[14:18], refs[18:]
    from_left, from_right, from_below, from_above = fars
    loads = [
        pltpu.make_async_copy(src, dst, sems.at[i])
        for i, (src, dst) in enumerate(
            zip((fm_hbm, *far_hbm, gm_hbm, gz_hbm), (fm_ref, *fars, gm_ref, gz_ref))
        )
    ]
    for c in loads:
        c.start()
    ins = (
        (from_above, 0), (from_above, 16), (from_above, 32), (from_right, 0),
        (from_left, 0), (from_below, 0), (from_below, 16), (from_below, 32),
    )

    def imported(d, row, h=slice(None)):
        ref, at = ins[d]
        return ref[row, at : at + 16, h]

    far = slice(64, 192)
    tl = lanes(192, 192)
    for k in range(9):
        oh3[k] = one_hot(cols_ref[:, k : k + 1] == tl)
    loads[0].wait()

    def own_z(x, _):
        for s in (0, 1):
            parts = pack_z(lambda y, h: fm_ref[8 * x + y, :, h], s == 0, 64)
            tz[s, x, 0:64, :] = jnp.concatenate(parts, axis=1).astype(BF16)
        return _

    lax.fori_loop(0, 8, own_z, 0, unroll=2)
    for c in loads[1:5]:
        c.wait()
    for row, (x, y) in enumerate(SHELL):
        places = []
        if x in (0, 7):
            places.append((xt, 0 if x == 7 else 1, y))
        if y in (0, 7):
            places.append((yt, 0 if y == 7 else 1, x))
        for ref, i, j in places:
            ref[i, j, 0:64, :] = fm_ref[8 * x + y]
            for d in range(8):
                ref[i, j, 64 + 16 * d : 80 + 16 * d, :] = imported(d, row)
    for i, x in enumerate((7, 0)):
        for s in (0, 1):
            parts = pack_z(lambda y, h: xt[i, y, far, h], s == 0, 128)
            tz[s, x, far, :] = jnp.concatenate(parts, axis=1).astype(BF16)

    def compact(row, h):
        return jnp.concatenate([imported(d, 28 + row, halves(h)) for d in range(8)], axis=0).astype(F32)

    sub = lanes(128) // 32
    for x in range(1, 7):
        for s in (0, 1):
            top = s == 0
            src = halves(1 if top else 0)
            first = unsqueeze(compact, 2 * (x - 1) + s, 0, 128)
            second = unsqueeze(compact, 2 * (x - 1) + s, 1, 128)
            y0 = roll(yt[1, x, far, src].astype(F32), -96 if top else 0)
            y7 = roll(yt[0, x, far, src].astype(F32), 96 - (96 if top else 0))
            first = jnp.where(sub == 0, y0, first)
            second = jnp.where(sub == 3, y7, second)
            tz[s, x, far, :] = jnp.concatenate([first, second], axis=1).astype(BF16)

    lane = lanes(64, 256)

    def halo_z(k, s, x, u):
        v = dot(oh3[k], tz[s, x])
        zero = jnp.zeros((64, 256), F32)
        a_ref[s, u] = v[64:128].astype(BF16)
        ax_ref[s, u] = jnp.where(
            lane >= 224, v[0:64], jnp.where(lane < 32, v[128:192], zero)
        ).astype(BF16)

    def fill(x, _):
        for y in range(8):
            vm_ref[x + 1, y + 1] = fm_ref[8 * x + y]
        vm_ref[x + 1, 0] = dot(oh3[4, 0:64, :], yt[0, x]).astype(BF16)
        vm_ref[x + 1, 9] = dot(oh3[4, 128:192, :], yt[1, x]).astype(BF16)
        for s in (0, 1):
            halo_z(3 + 2 * s, s, x, x + 1)
        return _

    lax.fori_loop(0, 8, fill, 0, unroll=UNROLL)
    for i, (u, x, ex) in enumerate(((0, 7, 0), (9, 0, 2))):
        def along(y, _, i=i, u=u, ex=ex):
            vm_ref[u, y + 1] = dot(oh3[3 * ex + 1, 64:128, :], xt[i, y]).astype(BF16)
            return _

        lax.fori_loop(0, 8, along, 0, unroll=UNROLL)
        vm_ref[u, 0] = dot(oh3[3 * ex + 1, 0:64, :], xt[i, 7]).astype(BF16)
        vm_ref[u, 9] = dot(oh3[3 * ex + 1, 128:192, :], xt[i, 0]).astype(BF16)
        for s in (0, 1):
            halo_z(3 * ex + 2 * s, s, x, u)

    stores = [
        pltpu.make_async_copy(src, dst, sems.at[7 + i])
        for i, (src, dst) in enumerate(zip((vm_ref, a_ref, ax_ref), (vm_hbm, a_hbm, ax_hbm)))
    ]
    for c in stores:
        c.start()
    for c in loads[5:]:
        c.wait()

    def tap(k, _):
        cols = vm_ref[pl.ds(k // 3, 8), pl.ds(k % 3, 8)].reshape(4096, 256)
        acc[k] = dot(gm_ref[...], cols)
        return _

    lax.fori_loop(0, 9, tap, 0)
    for s in (0, 1):
        for a in range(3):
            for i, r in enumerate((a_ref, ax_ref)):
                acc[9 + 6 * s + 2 * a + i] = dot(gz_ref[s], r[s, a : a + 8].reshape(512, 256))

    blk = lanes(32, 256) // 32

    def band_sum(k, r):
        total = None
        for i in range(8):
            if not 0 <= i + r - 1 < 8:
                continue
            v = acc[k, 32 * i : 32 * i + 32, :]
            v = jnp.where(blk == i + r - 1, v, jnp.zeros_like(v))
            total = v if total is None else total + v
        return total

    def fold_lanes(total):
        v = total[:, 0:128] + total[:, 128:256]
        v = v + pltpu.roll(v, 64, axis=1)
        return v + pltpu.roll(v, 32, axis=1)

    for a in range(3):
        for q in range(3):
            for r in range(3):
                total = band_sum(3 * a + q, r)
                if r != 1:
                    s = r // 2
                    base = 9 + 6 * s + 2 * a
                    total = total + band_sum(base, q)
                    if q == 0:
                        v = acc[base + 1, 0:32, :]
                        total = total + jnp.where(blk == 7, v, jnp.zeros_like(v))
                    if q == 2:
                        v = acc[base + 1, 224:256, :]
                        total = total + jnp.where(blk == 0, v, jnp.zeros_like(v))
                t = 9 * a + 3 * q + r
                fold[32 * t : 32 * t + 32, :] = fold_lanes(total)
    quarter = lanes(216) // 32
    v = fold[0:216, :]
    for k in range(1, 4):
        v = jnp.where(quarter == k, fold[216 * k : 216 * k + 216, :], v)
    dw_ref[0:216, :] = v
    dw_ref[216:224, :] = fold_lanes(bias_ref[...])
    for c in stores:
        c.wait()


def wgrad(fm, gm, gz, cols3, bias_sum, mark, arrived):
    sd = jax.ShapeDtypeStruct
    return pl.pallas_call(
        wgrad_kernel,
        out_shape=[
            sd((10, 10, 64, 256), BF16),
            sd((2, 10, 64, 256), BF16),
            sd((2, 10, 64, 256), BF16),
            sd((224, 128), F32),
        ],
        in_specs=[ANY] * 3 + [VMEM] * 2 + [ANY] * 5,
        out_specs=[ANY] * 3 + [VMEM],
        scratch_shapes=[pltpu.VMEM(v.shape, v.dtype) for v in (fm, gm, gz)]
        + [
            pltpu.VMEM((10, 10, 64, 256), BF16),
            pltpu.VMEM((2, 10, 64, 256), BF16),
            pltpu.VMEM((2, 10, 64, 256), BF16),
        ]
        + [pltpu.VMEM(v.shape, v.dtype) for v in arrived]
        + [
            pltpu.VMEM((2, 8, 192, 256), BF16),
            pltpu.VMEM((2, 8, 192, 256), BF16),
            pltpu.VMEM((2, 8, 192, 256), BF16),
            pltpu.VMEM((9, 192, 192), BF16),
            pltpu.VMEM((21, 256, 256), F32),
            pltpu.VMEM((864, 128), F32),
            DMA((10,)),
        ],
        compiler_params=PARAMS,
        cost_estimate=cost(16),
        name="wgrad",
    )(fm, gm, gz, cols3, bias_sum, mark, *arrived)


def forward_kernel(first, count_ref, vm_hbm, a_hbm, ax_hbm, bm_hbm, bym_hbm, bye_hbm, bias_ref, *refs):
    out_hbm, vm_ref, a_ref, ax_ref, bm_ref, bym_ref, bye_ref, es, os, ob, sems = refs[-11:]
    n = os.shape[0] // 8
    planes = pl.ds(first, n + 2)
    loads = [
        pltpu.make_async_copy(a_hbm.at[:, planes], a_ref, sems.at[0]),
        pltpu.make_async_copy(ax_hbm.at[:, planes], ax_ref, sems.at[1]),
        pltpu.make_async_copy(bym_hbm, bym_ref, sems.at[2]),
        pltpu.make_async_copy(bye_hbm, bye_ref, sems.at[3]),
        pltpu.make_async_copy(bm_hbm, bm_ref, sems.at[4]),
        pltpu.make_async_copy(vm_hbm.at[planes], vm_ref, sems.at[5]),
    ]
    for c in loads:
        c.start()
    count = count_ref[0, 0]
    live = (lax.broadcasted_iota(jnp.int32, (64, 256), 0) < count).astype(F32)
    for c in loads[:4]:
        c.wait()
    for s in (0, 1):
        total = None
        for a in range(3):
            for ref, band in ((a_ref, bym_ref), (ax_ref, bye_ref)):
                part = dot(ref[s, a : a + n].reshape(64 * n, 256), band[2 * a + s])
                total = part if total is None else total + part
        es[s] = total.reshape(n, 64, 256)
    bias = bias_ref[...]
    for c in loads[4:]:
        c.wait()

    def plane(x, _):
        cols = jnp.concatenate(
            [vm_ref[x + a, q : q + 8].reshape(512, 256) for a in range(3) for q in range(3)], axis=1
        )
        total = dot(cols, bm_ref[...].reshape(2304, 256)).reshape(8, 64, 256)
        for y in range(8):
            low, high = unpack_z(lambda h: es[0, x, :, h], lambda h: es[1, x, :, h], y, 64)
            v = total[y] + jnp.concatenate([low, high], axis=1) + bias
            os[8 * x + y] = (v * live).astype(BF16)
        return _

    def store(i):
        rows = pl.ds(16 * i + 8 * first, 16)
        return pltpu.make_async_copy(ob.at[:, pl.ds(16 * i, 16)], out_hbm.at[:, rows], sems.at[6 + i])

    def two(i, _):
        plane(2 * i, 0)
        plane(2 * i + 1, 0)
        ob[:, pl.ds(pl.multiple_of(16 * i, 16), 16), :] = jnp.transpose(
            os[pl.ds(pl.multiple_of(16 * i, 16), 16)], (1, 0, 2)
        )
        return _

    for i in range(n // 2):
        two(i, 0)
        store(i).start()
    for i in range(n // 2):
        store(i).wait()


def forward(first, n, count, vm, a, ax, bm, bym, bye, bias_row, before=None):
    more = [] if before is None else [before]
    return pl.pallas_call(
        functools.partial(forward_kernel, first),
        out_shape=jax.ShapeDtypeStruct((64, 64, 256), BF16),
        in_specs=[SMEM] + [ANY] * 6 + [VMEM] + [ANY] * len(more),
        out_specs=ANY,
        input_output_aliases={8: 0} if more else {},
        scratch_shapes=[
            pltpu.VMEM((n + 2, 10, 64, 256), BF16),
            pltpu.VMEM((2, n + 2, 64, 256), BF16),
            pltpu.VMEM((2, n + 2, 64, 256), BF16),
            pltpu.VMEM(bm.shape, BF16),
            pltpu.VMEM(bym.shape, BF16),
            pltpu.VMEM(bye.shape, BF16),
            pltpu.VMEM((2, n, 64, 256), F32),
            pltpu.VMEM((8 * n, 64, 256), BF16),
            pltpu.VMEM((64, 8 * n, 256), BF16),
            DMA((6 + n // 2,)),
        ],
        compiler_params=PARAMS,
        cost_estimate=cost(1),
        name="forward",
    )(count, vm, a, ax, bm, bym, bye, bias_row, *more)


def finish_kernel(count_ref, own_hbm, slots_ref, *refs):
    hbm, out_hbm, (zp, os, ob, own_ref) = refs[:4], refs[4], refs[5:9]
    far, sems = refs[9:13], refs[13]
    from_left, from_right, from_below, from_above = far
    loads = [
        pltpu.make_async_copy(src, dst, sems.at[i])
        for i, (src, dst) in enumerate(zip((*hbm, own_hbm), (*far, own_ref)))
    ]
    for c in loads:
        c.start()
    count = count_ref[0, 0]
    live = (lax.broadcasted_iota(jnp.int32, (64, 256), 0) < count).astype(F32)
    chosen = one_hot(slots_ref[...] == lax.broadcasted_iota(jnp.int32, (64, 128), 0))

    def back(row):
        return dot(
            chosen,
            jnp.concatenate(
                [from_below[row], from_left[row, 0:16], from_right[row, 0:16], from_above[row]],
                axis=0,
            ),
        )

    for c in loads:
        c.wait()
    for row, (x, y) in enumerate(SHELL):
        v = own_ref[8 * x + y] + back(row)
        os[8 * x + y] = (v * live).astype(BF16)
    for k in range(9):
        zp[k] = back(28 + k)

    def piece(x, s, h):
        return unsqueeze(lambda row, hh: zp[row, :, halves(hh)], 2 * (x - 1) + s, h, 64)

    for x in range(1, 7):
        parts = {(s, h): piece(x, s, h) for s in (0, 1) for h in (0, 1)}
        for y in range(1, 7):
            first, second = unpack_z(
                lambda h: parts[1, h.start // 128], lambda h: parts[0, h.start // 128], y, 64
            )
            v = own_ref[8 * x + y] + jnp.concatenate([first, second], axis=1)
            os[8 * x + y] = (v * live).astype(BF16)
    stores = []
    for i in range(4):
        rows = slice(16 * i, 16 * i + 16)
        ob[:, rows, :] = jnp.transpose(os[rows], (1, 0, 2))
        stores.append(pltpu.make_async_copy(ob.at[:, rows], out_hbm.at[:, rows], sems.at[5 + i]))
        stores[-1].start()
    for c in stores:
        c.wait()


def finish(count, own, slots_row, returned):
    return pl.pallas_call(
        finish_kernel,
        out_shape=jax.ShapeDtypeStruct((64, 64, 256), BF16),
        in_specs=[SMEM, ANY, VMEM] + [ANY] * 4,
        out_specs=ANY,
        scratch_shapes=[
            pltpu.VMEM((9, 64, 256), F32),
            pltpu.VMEM((64, 64, 256), BF16),
            pltpu.VMEM((64, 64, 256), BF16),
            pltpu.VMEM((64, 64, 256), F32),
        ]
        + [pltpu.VMEM(v.shape, BF16) for v in returned]
        + [DMA((9,))],
        compiler_params=PARAMS,
        cost_estimate=cost(5),
        name="finish",
    )(count, own, slots_row, *returned)


def shift(value, axis, by):
    n = lax.axis_size(axis)
    return lax.ppermute(value, axis, [(i, i + by) for i in range(n) if 0 <= i + by < n])


def group(*blocks):
    return jnp.concatenate(blocks, axis=1)


def sum_steps():
    def doubling(axis, n, by):
        return lambda v: v + lax.ppermute(v, axis, [(i, i ^ by) for i in range(n)])

    found = []
    for axis in ("tile", "space"):
        n = lax.axis_size(axis)
        if n & (n - 1):
            found.append([functools.partial(lax.psum, axis_name=axis)])
        else:
            found.append([doubling(axis, n, 1 << k) for k in range(n.bit_length() - 1)])
    return found


def local(features, weight, bias_vector, cotangent, counts, send_slots, neighbours):
    slots = send_slots[0, 0].reshape(1, 128)
    near = neighbours[0, 0]
    full = jnp.concatenate(
        [near[:, :13], jnp.full((64, 1), 192, jnp.int32), near[:, 13:]], axis=1
    ).reshape(64, 3, 3, 3)
    cols3 = jnp.transpose(full, (2, 0, 1, 3)).reshape(192, 9)
    rows3 = cols3.T
    rows2 = full[:, :, :, 1].reshape(64, 9).T
    rows2 = jnp.concatenate([rows2, rows2], axis=1)
    wt = jnp.tile(weight.reshape(27, 32, 32), (1, 1, 8))
    bias_row = jnp.tile(bias_vector, 8).reshape(1, 256)

    fm, right, left, down, up = pack(counts, features.reshape(64, 64, 256), slots.reshape(128, 1))
    from_left = shift(right, "tile", 1)
    from_right = shift(left, "tile", -1)
    go_up = group(from_right[:, 16:32], up, from_left[:, 16:32])
    go_down = group(from_right[:, 32:48], down, from_left[:, 32:48])
    go_up, go_down, cotangent = lax.optimization_barrier((go_up, go_down, cotangent))
    from_below = shift(go_up, "space", 1)
    from_above = shift(go_down, "space", -1)
    own, gm, gz, bm, bym, bye, bias_sum, to_left, to_right, below, above = dgrad(
        counts, cotangent.reshape(64, 64, 256), wt, rows3, rows2
    )
    back_right = shift(to_left, "tile", -1)
    back_left = shift(to_right, "tile", 1)
    mark = from_below[0, 0:16] + from_above[0, 0:16]
    mark, back_left, back_right = lax.optimization_barrier((mark, back_left, back_right))
    go_down = group(back_left[:, 16:32], below, back_right[:, 16:32])
    go_up = group(back_left[:, 32:48], above, back_right[:, 32:48])
    go_down, go_up, from_below, from_above = lax.optimization_barrier(
        (go_down, go_up, from_below, from_above)
    )
    back_above = shift(go_down, "space", -1)
    back_below = shift(go_up, "space", 1)
    vm, a, ax, dw = wgrad(fm, gm, gz, cols3, bias_sum, mark, (from_left, from_right, from_below, from_above))
    args = (counts, vm, a, ax, bm, bym, bye, bias_row)
    near, across = sum_steps()
    total = dw
    for step in near:
        total = step(total)
    out = forward(0, 8, *args)
    total, out, back_above, back_below = lax.optimization_barrier((total, out, back_above, back_below))
    grad_in = finish(counts, own, slots, (back_left, back_right, back_below, back_above))
    for i, step in enumerate(across):
        total = step(total)
        if i == 0:
            total, grad_in = lax.optimization_barrier((total, grad_in))

    scale = float(lax.axis_size("space") * lax.axis_size("tile") * 64 * 512) ** (-0.5)
    total = total * scale
    weight_grad = jnp.transpose(total[:216].reshape(216, 4, 32), (1, 0, 2)).reshape(27, 32, 32)
    weight_grad = jnp.transpose(weight_grad, (0, 2, 1)).reshape(3, 3, 3, 32, 32)
    bias_grad = jnp.sum(total[216:224, :32], axis=0)
    return out.reshape(features.shape), grad_in.reshape(features.shape), weight_grad, bias_grad


def solution(mesh):
    wide = P("space", "tile", None, None, None, None)
    return jax.shard_map(
        local,
        mesh=mesh,
        in_specs=(wide, P(), P(), wide, P("space", "tile"), P("space", "tile", None, None), P("space", "tile", None, None)),
        out_specs=(wide, wide, P(), P()),
        check_vma=False,
    )
```

```python
import functools

import jax
import jax.numpy as jnp
from jax import lax
from jax.experimental import pallas as pl
from jax.experimental.pallas import tpu as pltpu
from jax.sharding import PartitionSpec as P

F32 = jnp.float32
BF16 = jnp.bfloat16
DEVICE_SIDES = [(s, t) for s in (-1, 0, 1) for t in (-1, 0, 1) if (s, t) != (0, 0)]
SHELL = (
    [(0, y) for y in range(8)]
    + [(7, y) for y in range(8)]
    + [(x, 0) for x in range(1, 7)]
    + [(x, 7) for x in range(1, 7)]
)
ROWS = len(SHELL) + 9
UNROLL = 8
XS = 4
VMEM = pl.BlockSpec(memory_space=pltpu.VMEM)
SMEM = pl.BlockSpec(memory_space=pltpu.SMEM)
ANY = pl.BlockSpec(memory_space=pl.ANY)
DMA = pltpu.SemaphoreType.DMA
PARAMS = pltpu.CompilerParams(vmem_limit_bytes=56 * 1024 * 1024)


def cost(us):
    return pl.CostEstimate(flops=us * 10**6, bytes_accessed=us * 10**3, transcendentals=0)


def dot(a, b):
    return jnp.dot(a, b, preferred_element_type=F32)


def dot_nt(a, b):
    return lax.dot_general(a, b, (((1,), (1,)), ((), ())), preferred_element_type=F32)


def dot_tn(a, b):
    return lax.dot_general(a, b, (((0,), (0,)), ((), ())), preferred_element_type=F32)


def roll(v, by):
    by = by % 128
    return v if by == 0 else pltpu.roll(v, by, axis=1)


def lanes(n, width=128):
    return lax.broadcasted_iota(jnp.int32, (n, width), 1)


def one_hot(test):
    return jnp.where(test, 1.0, 0.0).astype(BF16)


def halves(h):
    return slice(128 * h, 128 * h + 128)


def pack_z(load, top, n, ys=range(8)):
    sub = lanes(n) // 32
    out = []
    for h in (0, 1):
        acc = None
        for k in range(4):
            y = 4 * h + k
            if y not in ys:
                continue
            v = load(y, halves(1 if top else 0)).astype(F32)
            v = roll(v, 32 * k - (96 if top else 0))
            acc = v if acc is None else jnp.where(sub == k, v, acc)
        out.append(acc)
    return out


def unpack_z(low, high, y, n):
    k = y % 4
    lane = lanes(n)
    zero = jnp.zeros((n, 128), F32)
    first = jnp.where(lane < 32, roll(low(halves(y // 4)), -32 * k), zero)
    second = jnp.where(lane >= 96, roll(high(halves(y // 4)), 96 - 32 * k), zero)
    return first, second


def squeeze(piece, g, k, h, n):
    lane = lanes(n)
    last = piece(4 * g + 3, h)
    if h == 0:
        return jnp.where(lane < 32, roll(last, -32 * (k + 1)), piece(4 * g + k, h))
    return jnp.where(lane >= 96, roll(last, 96 - 32 * k), piece(4 * g + k, h))


def unsqueeze(row, p, h, n):
    g, k = p // 4, p % 4
    if k < 3:
        return row(3 * g + k, h)
    sub = lanes(n) // 32
    acc = None
    for j in range(3):
        v = roll(row(3 * g + j, h), 32 * (j + 1) if h == 0 else 32 * j - 96)
        acc = v if acc is None else jnp.where(sub == (j + 1 if h == 0 else j), v, acc)
    return acc


def pack_kernel(count_ref, f_ref, slots_ref, fm_ref, right, left, down, up, zp):
    count = count_ref[0, 0]
    live = (lax.broadcasted_iota(jnp.int32, (64, 256), 0) < count).astype(F32)

    def mask_rows(i, _):
        rows = pl.ds(16 * i, 16)
        v = jnp.transpose(f_ref[:, rows, :], (1, 0, 2))
        fm_ref[rows] = v * live[None].astype(BF16)
        return _

    lax.fori_loop(0, 4, mask_rows, 0)
    chosen = one_hot(slots_ref[...] == lax.broadcasted_iota(jnp.int32, (128, 64), 1))

    def send(row, value):
        value = value.astype(BF16)
        for ref, order in ((right, (4, 7, 2)), (left, (3, 5, 0)), (down, (1,)), (up, (6,))):
            for i, d in enumerate(order):
                ref[row, 16 * i : 16 * i + 16, :] = value[16 * d : 16 * d + 16]

    for row, (x, y) in enumerate(SHELL):
        send(row, dot(chosen, fm_ref[8 * x + y]))
    for x in range(1, 7):
        for s in (0, 1):
            h0, h1 = pack_z(lambda y, h: fm_ref[8 * x + y, :, h], s == 0, 64, range(1, 7))
            z = jnp.concatenate([h0, h1], axis=1).astype(BF16)
            zp[2 * (x - 1) + s] = dot(chosen, z)
    for g in range(3):
        for k in range(3):
            parts = [
                squeeze(lambda p, hh: zp[p, :, halves(hh)], g, k, h, 128) for h in (0, 1)
            ]
            send(28 + 3 * g + k, jnp.concatenate(parts, axis=1))


def pack(count, f_rows, slots_col):
    return pl.pallas_call(
        pack_kernel,
        out_shape=[jax.ShapeDtypeStruct((64, 64, 256), BF16)]
        + [jax.ShapeDtypeStruct((ROWS, n, 256), BF16) for n in (48, 48, 16, 16)],
        in_specs=[SMEM, VMEM, VMEM],
        out_specs=[VMEM] * 5,
        scratch_shapes=[pltpu.VMEM((12, 128, 256), F32)],
        compiler_params=PARAMS,
        cost_estimate=cost(5),
        name="pack",
    )(count, f_rows, slots_col)


def build_bands(wt_ref, bm_ref, bym_ref, bye_ref):
    blk = lanes(32, 256) // 32
    zero = jnp.zeros((32, 256), F32)

    def banded(w0, w1, w2, i):
        row = jnp.where(blk == i - 1, w2, zero)
        row = jnp.where(blk == i, w1, row)
        return jnp.where(blk == i + 1, w0, row).astype(BF16)

    def one(aq, _):
        w0, w1, w2 = (wt_ref[3 * aq + r].astype(F32) for r in range(3))
        for i in range(8):
            bm_ref[aq, 32 * i : 32 * i + 32, :] = banded(w0, w1, w2, i)
        return _

    lax.fori_loop(0, 9, one, 0)

    def side(a, _):
        for s in (0, 1):
            w0, w1, w2 = (wt_ref[9 * a + 3 * q + 2 * s].astype(F32) for q in range(3))
            k = 2 * a + s
            for i in range(8):
                bym_ref[k, 32 * i : 32 * i + 32, :] = banded(w0, w1, w2, i)
            bye_ref[k] = jnp.zeros((256, 256), BF16)
            bye_ref[k, 0:32, :] = jnp.where(blk == 7, w2, zero).astype(BF16)
            bye_ref[k, 224:256, :] = jnp.where(blk == 0, w0, zero).astype(BF16)
        return _

    lax.fori_loop(0, 3, side, 0)


def high_low(v):
    high = v.astype(BF16)
    return high, (v - high.astype(F32)).astype(BF16)


def dgrad_kernel(
    count_ref, g_ref, wt_ref, rows3_ref, rows2_ref,
    own_hbm, gm_hbm, gz_hbm, bm_hbm, bym_hbm, bye_hbm, bias_ref, *refs
):
    to_left, to_right, below, above = refs[:4]
    own_ref, bm_ref, bym_ref, bye_ref, gt, gzt, gpad, gzpad, pg, ag, agx, xf, yf, tz, oht3, oht2, sems = refs[4:]
    count = count_ref[0, 0]
    build_bands(wt_ref, bm_ref, bym_ref, bye_ref)
    stores = [
        pltpu.make_async_copy(src, dst, sems.at[i])
        for i, (src, dst) in enumerate(
            (
                (bm_ref, bm_hbm),
                (bym_ref, bym_hbm),
                (bye_ref, bye_hbm),
                (gt, gm_hbm),
                (gzt, gz_hbm),
                (own_ref, own_hbm),
            )
        )
    ]
    for c in stores[:3]:
        c.start()
    live = (lax.broadcasted_iota(jnp.int32, (64, 256), 0) < count).astype(F32)
    for i in (0, 1, 10, 11):
        gpad[i] = jnp.zeros((8, 64, 256), BF16)
        gzpad[0, i] = jnp.zeros((64, 256), BF16)
        gzpad[1, i] = jnp.zeros((64, 256), BF16)
    pg[:, 0] = jnp.zeros((10, 64, 256), F32)
    pg[:, 9] = jnp.zeros((10, 64, 256), F32)

    def load_g(x, _):
        both = jnp.transpose(g_ref[:, pl.ds(16 * x, 16), :], (1, 0, 2)) * live[None].astype(BF16)
        gpad[pl.ds(2 * x + 2, 2)] = both.reshape(2, 8, 64, 256)
        for i in (0, 1):
            for s in (0, 1):
                parts = pack_z(lambda y, h: gpad[2 * x + i + 2, y, :, h], s == 1, 64)
                z = jnp.concatenate(parts, axis=1).astype(BF16)
                gzpad[s, 2 * x + i + 2] = z
        return _

    lax.fori_loop(0, 4, load_g, 0)
    bias = jnp.zeros((8, 256), F32)
    for x in range(8):
        g = gpad[x + 2].reshape(512, 256)
        gt[:, 512 * x : 512 * x + 512] = g.T
        bias = bias + jnp.sum(g.astype(F32).reshape(64, 8, 256), axis=0)
    bias_ref[...] = bias
    for s in (0, 1):
        gzt[s] = gzpad[s, 2:10].reshape(512, 256).T
    for c in stores[3:5]:
        c.start()
    tsub = lax.broadcasted_iota(jnp.int32, (192, 192), 0)
    tsub2 = lax.broadcasted_iota(jnp.int32, (192, 128), 0)
    for k in range(9):
        oht3[k] = one_hot(rows3_ref[k : k + 1, :] == tsub)
        oht2[k] = one_hot(rows2_ref[k : k + 1, :] == tsub2)

    def plane(u, _):
        for q in (1, 0, 2):
            acc = None
            for a in range(3):
                part = dot_nt(gpad[u + 2 - a].reshape(512, 256), bm_ref[3 * a + q])
                acc = part if acc is None else acc + part
            acc = acc.reshape(8, 64, 256)
            if q == 1:
                pg[u, 1:9] = acc
            elif q == 0:
                pg[u, 0:8] = pg[u, 0:8] + acc
            else:
                pg[u, 2:10] = pg[u, 2:10] + acc
        return _

    lax.fori_loop(0, 10, plane, 0)
    for s in (0, 1):
        main, extra = None, None
        for a in range(3):
            z = gzpad[s, 2 - a : 12 - a].reshape(640, 256)
            pm = dot_nt(z, bym_ref[2 * a + s])
            pe = dot_nt(z, bye_ref[2 * a + s])
            main = pm if main is None else main + pm
            extra = pe if extra is None else extra + pe
        ag[s] = main.reshape(10, 64, 256)
        agx[s] = extra.reshape(10, 64, 256)

    def spread(k, v):
        high, low = high_low(v)
        return dot(oht2[k], jnp.concatenate([high, low], axis=0))

    lane = lanes(64, 256)

    def spread_z(k, s, u):
        m, e = ag[s, u], agx[s, u]
        zero = jnp.zeros_like(e)
        v = jnp.concatenate(
            [jnp.where(lane >= 224, e, zero), m, jnp.where(lane < 32, e, zero)], axis=0
        )
        high, low = high_low(v)
        return dot(oht3[k], high) + dot(oht3[k], low)

    def inner(x, _):
        yf[0, x] = spread(3, pg[x + 1, 0])
        yf[1, x] = spread(5, pg[x + 1, 9])
        for s in (0, 1):
            tz[s, x] = spread_z(3 + 2 * s, s, x + 1)
        return _

    lax.fori_loop(0, 8, inner, 0, unroll=UNROLL)
    for i, (u, x, ex) in enumerate(((0, 7, 0), (9, 0, 2))):
        def along(y, _, i=i, u=u, ex=ex):
            xf[i, y] = spread(3 * ex + 1, pg[u, y + 1])
            return _

        lax.fori_loop(0, 8, along, 0, unroll=UNROLL)
        yf[0, x] = yf[0, x] + spread(3 * ex, pg[u, 0])
        yf[1, x] = yf[1, x] + spread(3 * ex + 2, pg[u, 9])
        for s in (0, 1):
            tz[s, x] = tz[s, x] + spread_z(3 * ex + 2 * s, s, u)

    def own(x, _):
        for y in range(8):
            first, second = unpack_z(
                lambda h: tz[1, x, 0:64, h], lambda h: tz[0, x, 0:64, h], y, 64
            )
            extra = jnp.concatenate([first, second], axis=1)
            v = pg[x + 1, y + 1] + extra
            if y == 7:
                v = v + yf[0, x, 0:64, :]
            if y == 0:
                v = v + yf[1, x, 0:64, :]
            own_ref[8 * x + y] = v
        return _

    lax.fori_loop(0, 8, own, 0)
    for i, x in enumerate((7, 0)):
        for y in range(8):
            own_ref[8 * x + y] = own_ref[8 * x + y] + xf[i, y, 0:64, :]

    stores[5].start()

    def give(row, value):
        value = value.astype(BF16)
        for ref, order in ((to_left, (4, 7, 2)), (to_right, (3, 5, 0)), (below, (6,)), (above, (1,))):
            for i, d in enumerate(order):
                ref[row, 16 * i : 16 * i + 16, :] = value[16 * d : 16 * d + 16]

    far = slice(64, 192)
    for row, (x, y) in enumerate(SHELL):
        first, second = unpack_z(lambda h: tz[1, x, far, h], lambda h: tz[0, x, far, h], y, 128)
        v = jnp.concatenate([first, second], axis=1)
        if x in (0, 7):
            v = v + xf[0 if x == 7 else 1, y, far, :]
        if y in (0, 7):
            v = v + yf[0 if y == 7 else 1, x, far, :]
        give(row, v)
    for g in range(3):
        for k in range(3):
            parts = [
                squeeze(lambda p, hh: tz[p % 2, 1 + p // 2, far, halves(hh)], g, k, h, 128)
                for h in (0, 1)
            ]
            give(28 + 3 * g + k, jnp.concatenate(parts, axis=1))
    for c in stores:
        c.wait()


def dgrad(count, g_rows, wt, rows3, rows2):
    sd = jax.ShapeDtypeStruct
    return pl.pallas_call(
        dgrad_kernel,
        out_shape=[
            sd((64, 64, 256), F32),
            sd((256, 4096), BF16),
            sd((2, 256, 512), BF16),
            sd((9, 256, 256), BF16),
            sd((6, 256, 256), BF16),
            sd((6, 256, 256), BF16),
            sd((8, 256), F32),
        ]
        + [sd((ROWS, n, 256), BF16) for n in (48, 48, 16, 16)],
        in_specs=[SMEM] + [VMEM] * 4,
        out_specs=[ANY] * 6 + [VMEM] * 5,
        scratch_shapes=[
            pltpu.VMEM((64, 64, 256), F32),
            pltpu.VMEM((9, 256, 256), BF16),
            pltpu.VMEM((6, 256, 256), BF16),
            pltpu.VMEM((6, 256, 256), BF16),
            pltpu.VMEM((256, 4096), BF16),
            pltpu.VMEM((2, 256, 512), BF16),
            pltpu.VMEM((12, 8, 64, 256), BF16),
            pltpu.VMEM((2, 12, 64, 256), BF16),
            pltpu.VMEM((10, 10, 64, 256), F32),
            pltpu.VMEM((2, 10, 64, 256), F32),
            pltpu.VMEM((2, 10, 64, 256), F32),
            pltpu.VMEM((2, 8, 192, 256), F32),
            pltpu.VMEM((2, 8, 192, 256), F32),
            pltpu.VMEM((2, 8, 192, 256), F32),
            pltpu.VMEM((9, 192, 192), BF16),
            pltpu.VMEM((9, 192, 128), BF16),
            DMA((6,)),
        ],
        compiler_params=PARAMS,
        cost_estimate=cost(20000),
        name="dgrad",
    )(count, g_rows, wt, rows3, rows2)


def halo_kernel(fm_hbm, cols_ref, *refs):
    far_hbm, (vm_hbm, a_hbm, ax_hbm) = refs[:4], refs[4:7]
    fm_ref, vm_ref, a_ref, ax_ref = refs[7:11]
    fars, (xt, yt, tz, oh3, sems) = refs[11:15], refs[15:]
    from_left, from_right, from_below, from_above = fars
    loads = [
        pltpu.make_async_copy(src, dst, sems.at[i])
        for i, (src, dst) in enumerate(zip((fm_hbm, *far_hbm), (fm_ref, *fars)))
    ]
    for c in loads:
        c.start()
    ins = (
        (from_above, 0), (from_above, 16), (from_above, 32), (from_right, 0),
        (from_left, 0), (from_below, 0), (from_below, 16), (from_below, 32),
    )

    def imported(d, row, h=slice(None)):
        ref, at = ins[d]
        return ref[row, at : at + 16, h]

    far = slice(64, 192)
    tl = lanes(192, 192)
    for k in range(9):
        oh3[k] = one_hot(cols_ref[:, k : k + 1] == tl)
    loads[0].wait()

    def own_z(x, _):
        for s in (0, 1):
            parts = pack_z(lambda y, h: fm_ref[8 * x + y, :, h], s == 0, 64)
            tz[s, x, 0:64, :] = jnp.concatenate(parts, axis=1).astype(BF16)
        return _

    lax.fori_loop(0, 8, own_z, 0, unroll=2)
    for c in loads[1:5]:
        c.wait()
    for row, (x, y) in enumerate(SHELL):
        places = []
        if x in (0, 7):
            places.append((xt, 0 if x == 7 else 1, y))
        if y in (0, 7):
            places.append((yt, 0 if y == 7 else 1, x))
        for ref, i, j in places:
            ref[i, j, 0:64, :] = fm_ref[8 * x + y]
            for d in range(8):
                ref[i, j, 64 + 16 * d : 80 + 16 * d, :] = imported(d, row)
    for i, x in enumerate((7, 0)):
        for s in (0, 1):
            parts = pack_z(lambda y, h: xt[i, y, far, h], s == 0, 128)
            tz[s, x, far, :] = jnp.concatenate(parts, axis=1).astype(BF16)

    def compact(row, h):
        return jnp.concatenate([imported(d, 28 + row, halves(h)) for d in range(8)], axis=0).astype(F32)

    sub = lanes(128) // 32
    for x in range(1, 7):
        for s in (0, 1):
            top = s == 0
            src = halves(1 if top else 0)
            first = unsqueeze(compact, 2 * (x - 1) + s, 0, 128)
            second = unsqueeze(compact, 2 * (x - 1) + s, 1, 128)
            y0 = roll(yt[1, x, far, src].astype(F32), -96 if top else 0)
            y7 = roll(yt[0, x, far, src].astype(F32), 96 - (96 if top else 0))
            first = jnp.where(sub == 0, y0, first)
            second = jnp.where(sub == 3, y7, second)
            tz[s, x, far, :] = jnp.concatenate([first, second], axis=1).astype(BF16)

    lane = lanes(64, 256)

    def halo_z(k, s, x, u):
        v = dot(oh3[k], tz[s, x])
        zero = jnp.zeros((64, 256), F32)
        a_ref[s, u] = v[64:128].astype(BF16)
        ax_ref[s, u] = jnp.where(
            lane >= 224, v[0:64], jnp.where(lane < 32, v[128:192], zero)
        ).astype(BF16)

    def fill(x, _):
        for y in range(8):
            vm_ref[x + 1, y + 1] = fm_ref[8 * x + y]
        vm_ref[x + 1, 0] = dot(oh3[4, 0:64, :], yt[0, x]).astype(BF16)
        vm_ref[x + 1, 9] = dot(oh3[4, 128:192, :], yt[1, x]).astype(BF16)
        for s in (0, 1):
            halo_z(3 + 2 * s, s, x, x + 1)
        return _

    lax.fori_loop(0, 8, fill, 0, unroll=UNROLL)
    for i, (u, x, ex) in enumerate(((0, 7, 0), (9, 0, 2))):
        def along(y, _, i=i, u=u, ex=ex):
            vm_ref[u, y + 1] = dot(oh3[3 * ex + 1, 64:128, :], xt[i, y]).astype(BF16)
            return _

        lax.fori_loop(0, 8, along, 0, unroll=UNROLL)
        vm_ref[u, 0] = dot(oh3[3 * ex + 1, 0:64, :], xt[i, 7]).astype(BF16)
        vm_ref[u, 9] = dot(oh3[3 * ex + 1, 128:192, :], xt[i, 0]).astype(BF16)
        for s in (0, 1):
            halo_z(3 * ex + 2 * s, s, x, u)

    stores = [
        pltpu.make_async_copy(src, dst, sems.at[5 + i])
        for i, (src, dst) in enumerate(zip((vm_ref, a_ref, ax_ref), (vm_hbm, a_hbm, ax_hbm)))
    ]
    for c in stores:
        c.start()
    for c in stores:
        c.wait()


def halo(fm, cols3, arrived):
    sd = jax.ShapeDtypeStruct
    edges = [(10, 10, 64, 256), (2, 10, 64, 256), (2, 10, 64, 256)]
    return pl.pallas_call(
        halo_kernel,
        out_shape=[sd(v, BF16) for v in edges],
        in_specs=[ANY, VMEM] + [ANY] * 4,
        out_specs=[ANY] * 3,
        scratch_shapes=[pltpu.VMEM(v, BF16) for v in [fm.shape, *edges, *(v.shape for v in arrived)]]
        + [pltpu.VMEM((2, 8, 192, 256), BF16)] * 3
        + [pltpu.VMEM((9, 192, 192), BF16), DMA((8,))],
        compiler_params=PARAMS,
        cost_estimate=cost(1),
        name="halo",
    )(fm, cols3, *arrived)


def wgrad_kernel(*refs):
    hbm, bias_ref, dw_ref = refs[:5], refs[5], refs[6]
    vm_ref, a_ref, ax_ref, gm_ref, gz_ref = refs[7:12]
    acc, fold, sems = refs[12:]
    loads = [
        pltpu.make_async_copy(src, dst, sems.at[i])
        for i, (src, dst) in enumerate(zip(hbm, refs[7:12]))
    ]
    for c in loads:
        c.start()
    for c in (loads[0], loads[3]):
        c.wait()

    def tap(k, _):
        cols = vm_ref[pl.ds(k // 3, 8), pl.ds(k % 3, 8)].reshape(4096, 256)
        acc[k] = dot(gm_ref[...], cols)
        return _

    lax.fori_loop(0, 9, tap, 0)
    for c in (loads[1], loads[2], loads[4]):
        c.wait()
    for s in (0, 1):
        for a in range(3):
            for i, r in enumerate((a_ref, ax_ref)):
                acc[9 + 6 * s + 2 * a + i] = dot(gz_ref[s], r[s, a : a + 8].reshape(512, 256))

    blk = lanes(32, 256) // 32

    def band_sum(k, r):
        total = None
        for i in range(8):
            if not 0 <= i + r - 1 < 8:
                continue
            v = acc[k, 32 * i : 32 * i + 32, :]
            v = jnp.where(blk == i + r - 1, v, jnp.zeros_like(v))
            total = v if total is None else total + v
        return total

    def fold_lanes(total):
        v = total[:, 0:128] + total[:, 128:256]
        v = v + pltpu.roll(v, 64, axis=1)
        return v + pltpu.roll(v, 32, axis=1)

    for a in range(3):
        for q in range(3):
            for r in range(3):
                total = band_sum(3 * a + q, r)
                if r != 1:
                    s = r // 2
                    base = 9 + 6 * s + 2 * a
                    total = total + band_sum(base, q)
                    if q == 0:
                        v = acc[base + 1, 0:32, :]
                        total = total + jnp.where(blk == 7, v, jnp.zeros_like(v))
                    if q == 2:
                        v = acc[base + 1, 224:256, :]
                        total = total + jnp.where(blk == 0, v, jnp.zeros_like(v))
                t = 9 * a + 3 * q + r
                fold[32 * t : 32 * t + 32, :] = fold_lanes(total)
    quarter = lanes(216) // 32
    v = fold[0:216, :]
    for k in range(1, 4):
        v = jnp.where(quarter == k, fold[216 * k : 216 * k + 216, :], v)
    dw_ref[0:216, :] = v
    dw_ref[216:224, :] = fold_lanes(bias_ref[...])


def wgrad(vm, a, ax, gm, gz, bias_sum):
    return pl.pallas_call(
        wgrad_kernel,
        out_shape=jax.ShapeDtypeStruct((224, 128), F32),
        in_specs=[ANY] * 5 + [VMEM],
        out_specs=VMEM,
        scratch_shapes=[pltpu.VMEM(v.shape, v.dtype) for v in (vm, a, ax, gm, gz)]
        + [pltpu.VMEM((21, 256, 256), F32), pltpu.VMEM((864, 128), F32), DMA((5,))],
        compiler_params=PARAMS,
        cost_estimate=cost(1),
        name="wgrad",
    )(vm, a, ax, gm, gz, bias_sum)


def forward_kernel(first, count_ref, vm_hbm, a_hbm, ax_hbm, bm_hbm, bym_hbm, bye_hbm, bias_ref, *refs):
    out_hbm, vm_ref, a_ref, ax_ref, bm_ref, bym_ref, bye_ref, es, os, ob, sems = refs[-11:]
    n = os.shape[0] // 8
    planes = pl.ds(first, n + 2)
    loads = [
        pltpu.make_async_copy(a_hbm.at[:, planes], a_ref, sems.at[0]),
        pltpu.make_async_copy(ax_hbm.at[:, planes], ax_ref, sems.at[1]),
        pltpu.make_async_copy(bym_hbm, bym_ref, sems.at[2]),
        pltpu.make_async_copy(bye_hbm, bye_ref, sems.at[3]),
        pltpu.make_async_copy(bm_hbm, bm_ref, sems.at[4]),
        pltpu.make_async_copy(vm_hbm.at[planes], vm_ref, sems.at[5]),
    ]
    for c in loads:
        c.start()
    count = count_ref[0, 0]
    live = (lax.broadcasted_iota(jnp.int32, (64, 256), 0) < count).astype(F32)
    for c in loads[:4]:
        c.wait()
    for s in (0, 1):
        total = None
        for a in range(3):
            for ref, band in ((a_ref, bym_ref), (ax_ref, bye_ref)):
                part = dot(ref[s, a : a + n].reshape(64 * n, 256), band[2 * a + s])
                total = part if total is None else total + part
        es[s] = total.reshape(n, 64, 256)
    bias = bias_ref[...]
    for c in loads[4:]:
        c.wait()

    def plane(x, _):
        cols = jnp.concatenate(
            [vm_ref[x + a, q : q + 8].reshape(512, 256) for a in range(3) for q in range(3)], axis=1
        )
        total = dot(cols, bm_ref[...].reshape(2304, 256)).reshape(8, 64, 256)
        for y in range(8):
            low, high = unpack_z(lambda h: es[0, x, :, h], lambda h: es[1, x, :, h], y, 64)
            v = total[y] + jnp.concatenate([low, high], axis=1) + bias
            os[8 * x + y] = (v * live).astype(BF16)
        return _

    def store(i):
        rows = pl.ds(16 * i + 8 * first, 16)
        return pltpu.make_async_copy(ob.at[:, pl.ds(16 * i, 16)], out_hbm.at[:, rows], sems.at[6 + i])

    def two(i, _):
        plane(2 * i, 0)
        plane(2 * i + 1, 0)
        ob[:, pl.ds(pl.multiple_of(16 * i, 16), 16), :] = jnp.transpose(
            os[pl.ds(pl.multiple_of(16 * i, 16), 16)], (1, 0, 2)
        )
        return _

    for i in range(n // 2):
        two(i, 0)
        store(i).start()
    for i in range(n // 2):
        store(i).wait()


def forward(first, n, count, vm, a, ax, bm, bym, bye, bias_row, before=None):
    more = [] if before is None else [before]
    return pl.pallas_call(
        functools.partial(forward_kernel, first),
        out_shape=jax.ShapeDtypeStruct((64, 64, 256), BF16),
        in_specs=[SMEM] + [ANY] * 6 + [VMEM] + [ANY] * len(more),
        out_specs=ANY,
        input_output_aliases={8: 0} if more else {},
        scratch_shapes=[
            pltpu.VMEM((n + 2, 10, 64, 256), BF16),
            pltpu.VMEM((2, n + 2, 64, 256), BF16),
            pltpu.VMEM((2, n + 2, 64, 256), BF16),
            pltpu.VMEM(bm.shape, BF16),
            pltpu.VMEM(bym.shape, BF16),
            pltpu.VMEM(bye.shape, BF16),
            pltpu.VMEM((2, n, 64, 256), F32),
            pltpu.VMEM((8 * n, 64, 256), BF16),
            pltpu.VMEM((64, 8 * n, 256), BF16),
            DMA((6 + n // 2,)),
        ],
        compiler_params=PARAMS,
        cost_estimate=cost(1),
        name="forward",
    )(count, vm, a, ax, bm, bym, bye, bias_row, *more)


def finish_kernel(count_ref, own_hbm, slots_ref, *refs):
    hbm, out_hbm, (zp, os, ob, own_ref) = refs[:4], refs[4], refs[5:9]
    far, sems = refs[9:13], refs[13]
    from_left, from_right, from_below, from_above = far
    loads = [
        pltpu.make_async_copy(src, dst, sems.at[i])
        for i, (src, dst) in enumerate(zip((*hbm, own_hbm), (*far, own_ref)))
    ]
    for c in loads:
        c.start()
    count = count_ref[0, 0]
    live = (lax.broadcasted_iota(jnp.int32, (64, 256), 0) < count).astype(F32)
    chosen = one_hot(slots_ref[...] == lax.broadcasted_iota(jnp.int32, (64, 128), 0))

    def back(row):
        return dot(
            chosen,
            jnp.concatenate(
                [from_below[row], from_left[row, 0:16], from_right[row, 0:16], from_above[row]],
                axis=0,
            ),
        )

    for c in loads:
        c.wait()
    for row, (x, y) in enumerate(SHELL):
        v = own_ref[8 * x + y] + back(row)
        os[8 * x + y] = (v * live).astype(BF16)
    for k in range(9):
        zp[k] = back(28 + k)

    def piece(x, s, h):
        return unsqueeze(lambda row, hh: zp[row, :, halves(hh)], 2 * (x - 1) + s, h, 64)

    for x in range(1, 7):
        parts = {(s, h): piece(x, s, h) for s in (0, 1) for h in (0, 1)}
        for y in range(1, 7):
            first, second = unpack_z(
                lambda h: parts[1, h.start // 128], lambda h: parts[0, h.start // 128], y, 64
            )
            v = own_ref[8 * x + y] + jnp.concatenate([first, second], axis=1)
            os[8 * x + y] = (v * live).astype(BF16)
    stores = []
    for i in range(4):
        rows = slice(16 * i, 16 * i + 16)
        ob[:, rows, :] = jnp.transpose(os[rows], (1, 0, 2))
        stores.append(pltpu.make_async_copy(ob.at[:, rows], out_hbm.at[:, rows], sems.at[5 + i]))
        stores[-1].start()
    for c in stores:
        c.wait()


def finish(count, own, slots_row, returned):
    return pl.pallas_call(
        finish_kernel,
        out_shape=jax.ShapeDtypeStruct((64, 64, 256), BF16),
        in_specs=[SMEM, ANY, VMEM] + [ANY] * 4,
        out_specs=ANY,
        scratch_shapes=[
            pltpu.VMEM((9, 64, 256), F32),
            pltpu.VMEM((64, 64, 256), BF16),
            pltpu.VMEM((64, 64, 256), BF16),
            pltpu.VMEM((64, 64, 256), F32),
        ]
        + [pltpu.VMEM(v.shape, BF16) for v in returned]
        + [DMA((9,))],
        compiler_params=PARAMS,
        cost_estimate=cost(5),
        name="finish",
    )(count, own, slots_row, *returned)


def shift(value, axis, by):
    n = lax.axis_size(axis)
    return lax.ppermute(value, axis, [(i, i + by) for i in range(n) if 0 <= i + by < n])


def group(*blocks):
    return jnp.concatenate(blocks, axis=1)


def sum_steps():
    def doubling(axis, n, by):
        return lambda v: v + lax.ppermute(v, axis, [(i, i ^ by) for i in range(n)])

    def fourfold(axis, n, by):
        def step(v):
            a, b, c = (lax.ppermute(v, axis, [(i, i ^ (k * by)) for i in range(n)]) for k in (1, 2, 3))
            return (v + a) + (b + c)

        return step

    found = []
    for axis in ("tile", "space"):
        n = lax.axis_size(axis)
        if n & (n - 1):
            found.append([functools.partial(lax.psum, axis_name=axis)])
        else:
            bits = n.bit_length() - 1
            found.append([])
            if bits % 2 or axis == "space":
                found[-1].append(doubling(axis, n, 1))
            k = len(found[-1])
            while k < bits:
                found[-1].append((doubling if k + 1 == bits else fourfold)(axis, n, 1 << k))
                k += 2
    near, across = found
    return near + across[1:], across[:1]


def local(features, weight, bias_vector, cotangent, counts, send_slots, neighbours):
    slots = send_slots[0, 0].reshape(1, 128)
    near = neighbours[0, 0]
    full = jnp.concatenate(
        [near[:, :13], jnp.full((64, 1), 192, jnp.int32), near[:, 13:]], axis=1
    ).reshape(64, 3, 3, 3)
    cols3 = jnp.transpose(full, (2, 0, 1, 3)).reshape(192, 9)
    rows3 = cols3.T
    rows2 = full[:, :, :, 1].reshape(64, 9).T
    rows2 = jnp.concatenate([rows2, rows2], axis=1)
    wt = jnp.tile(weight.reshape(27, 32, 32), (1, 1, 8))
    bias_row = jnp.tile(bias_vector, 8).reshape(1, 256)

    fm, right, left, down, up = pack(counts, features.reshape(64, 64, 256), slots.reshape(128, 1))
    from_left = shift(right, "tile", 1)
    from_right = shift(left, "tile", -1)
    go_up = group(from_right[:, 16:32], up, from_left[:, 16:32])
    go_down = group(from_right[:, 32:48], down, from_left[:, 32:48])
    go_up, go_down, cotangent = lax.optimization_barrier((go_up, go_down, cotangent))
    from_below = shift(go_up, "space", 1)
    from_above = shift(go_down, "space", -1)
    own, gm, gz, bm, bym, bye, bias_sum, to_left, to_right, below, above = dgrad(
        counts, cotangent.reshape(64, 64, 256), wt, rows3, rows2
    )
    back_right = shift(to_left, "tile", -1)
    back_left = shift(to_right, "tile", 1)
    vm, a, ax = halo(fm, cols3, (from_left, from_right, from_below, from_above))
    vm, back_left, back_right = lax.optimization_barrier((vm, back_left, back_right))
    go_down = group(back_left[:, 16:32], below, back_right[:, 16:32])
    go_up = group(back_left[:, 32:48], above, back_right[:, 32:48])
    go_down, go_up, vm = lax.optimization_barrier((go_down, go_up, vm))
    back_above = shift(go_down, "space", -1)
    back_below = shift(go_up, "space", 1)
    dw = wgrad(vm, a, ax, gm, gz, bias_sum)
    args = (counts, vm, a, ax, bm, bym, bye, bias_row)
    near, across = sum_steps()
    total = dw
    for step in near:
        total = step(total)
    out = forward(0, 8, *args)
    total, out, back_above, back_below = lax.optimization_barrier((total, out, back_above, back_below))
    grad_in = finish(counts, own, slots, (back_left, back_right, back_below, back_above))
    for step in across:
        total = step(total)
    scale = float(lax.axis_size("space") * lax.axis_size("tile") * 64 * 512) ** (-0.5)
    total = total * scale
    weight_grad = jnp.transpose(total[:216].reshape(216, 4, 32), (1, 0, 2)).reshape(27, 32, 32)
    weight_grad = jnp.transpose(weight_grad, (0, 2, 1)).reshape(3, 3, 3, 32, 32)
    bias_grad = jnp.sum(total[216:224, :32], axis=0)
    return out.reshape(features.shape), grad_in.reshape(features.shape), weight_grad, bias_grad


def solution(mesh):
    wide = P("space", "tile", None, None, None, None)
    return jax.shard_map(
        local,
        mesh=mesh,
        in_specs=(wide, P(), P(), wide, P("space", "tile"), P("space", "tile", None, None), P("space", "tile", None, None)),
        out_specs=(wide, wide, P(), P()),
        check_vma=False,
    )
```

```python
import functools

import jax
import jax.numpy as jnp
from jax import lax
from jax.experimental import pallas as pl
from jax.experimental.pallas import tpu as pltpu
from jax.sharding import PartitionSpec as P

F32 = jnp.float32
BF16 = jnp.bfloat16
DEVICE_SIDES = [(s, t) for s in (-1, 0, 1) for t in (-1, 0, 1) if (s, t) != (0, 0)]
SHELL = (
    [(0, y) for y in range(8)]
    + [(7, y) for y in range(8)]
    + [(x, 0) for x in range(1, 7)]
    + [(x, 7) for x in range(1, 7)]
)
ROWS = len(SHELL) + 9
UNROLL = 8
XS = 4
VMEM = pl.BlockSpec(memory_space=pltpu.VMEM)
SMEM = pl.BlockSpec(memory_space=pltpu.SMEM)
ANY = pl.BlockSpec(memory_space=pl.ANY)
DMA = pltpu.SemaphoreType.DMA
PARAMS = pltpu.CompilerParams(vmem_limit_bytes=56 * 1024 * 1024)


def cost(us):
    return pl.CostEstimate(flops=us * 10**6, bytes_accessed=us * 10**3, transcendentals=0)


def dot(a, b):
    return jnp.dot(a, b, preferred_element_type=F32)


def dot_nt(a, b):
    return lax.dot_general(a, b, (((1,), (1,)), ((), ())), preferred_element_type=F32)


def dot_tn(a, b):
    return lax.dot_general(a, b, (((0,), (0,)), ((), ())), preferred_element_type=F32)


def roll(v, by):
    by = by % 128
    return v if by == 0 else pltpu.roll(v, by, axis=1)


def lanes(n, width=128):
    return lax.broadcasted_iota(jnp.int32, (n, width), 1)


def one_hot(test):
    return jnp.where(test, 1.0, 0.0).astype(BF16)


def halves(h):
    return slice(128 * h, 128 * h + 128)


def pack_z(load, top, n, ys=range(8)):
    sub = lanes(n) // 32
    out = []
    for h in (0, 1):
        acc = None
        for k in range(4):
            y = 4 * h + k
            if y not in ys:
                continue
            v = load(y, halves(1 if top else 0)).astype(F32)
            v = roll(v, 32 * k - (96 if top else 0))
            acc = v if acc is None else jnp.where(sub == k, v, acc)
        out.append(acc)
    return out


def unpack_z(low, high, y, n):
    k = y % 4
    lane = lanes(n)
    zero = jnp.zeros((n, 128), F32)
    first = jnp.where(lane < 32, roll(low(halves(y // 4)), -32 * k), zero)
    second = jnp.where(lane >= 96, roll(high(halves(y // 4)), 96 - 32 * k), zero)
    return first, second


def squeeze(piece, g, k, h, n):
    lane = lanes(n)
    last = piece(4 * g + 3, h)
    if h == 0:
        return jnp.where(lane < 32, roll(last, -32 * (k + 1)), piece(4 * g + k, h))
    return jnp.where(lane >= 96, roll(last, 96 - 32 * k), piece(4 * g + k, h))


def unsqueeze(row, p, h, n):
    g, k = p // 4, p % 4
    if k < 3:
        return row(3 * g + k, h)
    sub = lanes(n) // 32
    acc = None
    for j in range(3):
        v = roll(row(3 * g + j, h), 32 * (j + 1) if h == 0 else 32 * j - 96)
        acc = v if acc is None else jnp.where(sub == (j + 1 if h == 0 else j), v, acc)
    return acc


def pack_kernel(count_ref, f_ref, slots_ref, fm_ref, right, left, down, up, zp):
    count = count_ref[0, 0]
    live = (lax.broadcasted_iota(jnp.int32, (64, 256), 0) < count).astype(F32)

    def mask_rows(i, _):
        rows = pl.ds(16 * i, 16)
        v = jnp.transpose(f_ref[:, rows, :], (1, 0, 2))
        fm_ref[rows] = v * live[None].astype(BF16)
        return _

    lax.fori_loop(0, 4, mask_rows, 0)
    chosen = one_hot(slots_ref[...] == lax.broadcasted_iota(jnp.int32, (128, 64), 1))

    def send(row, value):
        value = value.astype(BF16)
        for ref, order in ((right, (4, 7, 2)), (left, (3, 5, 0)), (down, (1,)), (up, (6,))):
            for i, d in enumerate(order):
                ref[row, 16 * i : 16 * i + 16, :] = value[16 * d : 16 * d + 16]

    for row, (x, y) in enumerate(SHELL):
        send(row, dot(chosen, fm_ref[8 * x + y]))
    for x in range(1, 7):
        for s in (0, 1):
            h0, h1 = pack_z(lambda y, h: fm_ref[8 * x + y, :, h], s == 0, 64, range(1, 7))
            z = jnp.concatenate([h0, h1], axis=1).astype(BF16)
            zp[2 * (x - 1) + s] = dot(chosen, z)
    for g in range(3):
        for k in range(3):
            parts = [
                squeeze(lambda p, hh: zp[p, :, halves(hh)], g, k, h, 128) for h in (0, 1)
            ]
            send(28 + 3 * g + k, jnp.concatenate(parts, axis=1))


def pack(count, f_rows, slots_col):
    return pl.pallas_call(
        pack_kernel,
        out_shape=[jax.ShapeDtypeStruct((64, 64, 256), BF16)]
        + [jax.ShapeDtypeStruct((ROWS, n, 256), BF16) for n in (48, 48, 16, 16)],
        in_specs=[SMEM, VMEM, VMEM],
        out_specs=[VMEM] * 5,
        scratch_shapes=[pltpu.VMEM((12, 128, 256), F32)],
        compiler_params=PARAMS,
        cost_estimate=cost(5),
        name="pack",
    )(count, f_rows, slots_col)


def build_bands(wt_ref, bm_ref, bym_ref, bye_ref):
    blk = lanes(32, 256) // 32
    zero = jnp.zeros((32, 256), F32)

    def banded(w0, w1, w2, i):
        row = jnp.where(blk == i - 1, w2, zero)
        row = jnp.where(blk == i, w1, row)
        return jnp.where(blk == i + 1, w0, row).astype(BF16)

    def one(aq, _):
        w0, w1, w2 = (wt_ref[3 * aq + r].astype(F32) for r in range(3))
        for i in range(8):
            bm_ref[aq, 32 * i : 32 * i + 32, :] = banded(w0, w1, w2, i)
        return _

    lax.fori_loop(0, 9, one, 0)

    def side(a, _):
        for s in (0, 1):
            w0, w1, w2 = (wt_ref[9 * a + 3 * q + 2 * s].astype(F32) for q in range(3))
            k = 2 * a + s
            for i in range(8):
                bym_ref[k, 32 * i : 32 * i + 32, :] = banded(w0, w1, w2, i)
            bye_ref[k] = jnp.zeros((256, 256), BF16)
            bye_ref[k, 0:32, :] = jnp.where(blk == 7, w2, zero).astype(BF16)
            bye_ref[k, 224:256, :] = jnp.where(blk == 0, w0, zero).astype(BF16)
        return _

    lax.fori_loop(0, 3, side, 0)


def high_low(v):
    high = v.astype(BF16)
    return high, (v - high.astype(F32)).astype(BF16)


def dgrad_kernel(
    count_ref, g_ref, wt_ref, rows3_ref, rows2_ref,
    own_hbm, gm_hbm, gz_hbm, bm_hbm, bym_hbm, bye_hbm, bias_ref, *refs
):
    to_left, to_right, below, above = refs[:4]
    own_ref, bm_ref, bym_ref, bye_ref, gt, gzt, gpad, gzpad, pg, ag, agx, xf, yf, tz, oht3, oht2, sems = refs[4:]
    count = count_ref[0, 0]
    build_bands(wt_ref, bm_ref, bym_ref, bye_ref)
    stores = [
        pltpu.make_async_copy(src, dst, sems.at[i])
        for i, (src, dst) in enumerate(
            (
                (bm_ref, bm_hbm),
                (bym_ref, bym_hbm),
                (bye_ref, bye_hbm),
                (gt, gm_hbm),
                (gzt, gz_hbm),
                (own_ref, own_hbm),
            )
        )
    ]
    for c in stores[:3]:
        c.start()
    live = (lax.broadcasted_iota(jnp.int32, (64, 256), 0) < count).astype(F32)
    for i in (0, 1, 10, 11):
        gpad[i] = jnp.zeros((8, 64, 256), BF16)
        gzpad[0, i] = jnp.zeros((64, 256), BF16)
        gzpad[1, i] = jnp.zeros((64, 256), BF16)
    pg[:, 0] = jnp.zeros((10, 64, 256), F32)
    pg[:, 9] = jnp.zeros((10, 64, 256), F32)

    def load_g(x, _):
        both = jnp.transpose(g_ref[:, pl.ds(16 * x, 16), :], (1, 0, 2)) * live[None].astype(BF16)
        gpad[pl.ds(2 * x + 2, 2)] = both.reshape(2, 8, 64, 256)
        for i in (0, 1):
            for s in (0, 1):
                parts = pack_z(lambda y, h: gpad[2 * x + i + 2, y, :, h], s == 1, 64)
                z = jnp.concatenate(parts, axis=1).astype(BF16)
                gzpad[s, 2 * x + i + 2] = z
        return _

    lax.fori_loop(0, 4, load_g, 0)
    bias = jnp.zeros((8, 256), F32)
    for x in range(8):
        g = gpad[x + 2].reshape(512, 256)
        gt[:, 512 * x : 512 * x + 512] = g.T
        bias = bias + jnp.sum(g.astype(F32).reshape(64, 8, 256), axis=0)
    bias_ref[...] = bias
    for s in (0, 1):
        gzt[s] = gzpad[s, 2:10].reshape(512, 256).T
    for c in stores[3:5]:
        c.start()
    tsub = lax.broadcasted_iota(jnp.int32, (192, 192), 0)
    tsub2 = lax.broadcasted_iota(jnp.int32, (192, 128), 0)
    for k in range(9):
        oht3[k] = one_hot(rows3_ref[k : k + 1, :] == tsub)
        oht2[k] = one_hot(rows2_ref[k : k + 1, :] == tsub2)

    def plane(u, _):
        for q in (1, 0, 2):
            acc = None
            for a in range(3):
                part = dot_nt(gpad[u + 2 - a].reshape(512, 256), bm_ref[3 * a + q])
                acc = part if acc is None else acc + part
            acc = acc.reshape(8, 64, 256)
            if q == 1:
                pg[u, 1:9] = acc
            elif q == 0:
                pg[u, 0:8] = pg[u, 0:8] + acc
            else:
                pg[u, 2:10] = pg[u, 2:10] + acc
        return _

    lax.fori_loop(0, 10, plane, 0)
    for s in (0, 1):
        main, extra = None, None
        for a in range(3):
            z = gzpad[s, 2 - a : 12 - a].reshape(640, 256)
            pm = dot_nt(z, bym_ref[2 * a + s])
            pe = dot_nt(z, bye_ref[2 * a + s])
            main = pm if main is None else main + pm
            extra = pe if extra is None else extra + pe
        ag[s] = main.reshape(10, 64, 256)
        agx[s] = extra.reshape(10, 64, 256)

    def spread(k, v):
        high, low = high_low(v)
        return dot(oht2[k], jnp.concatenate([high, low], axis=0))

    lane = lanes(64, 256)

    def spread_z(k, s, u):
        m, e = ag[s, u], agx[s, u]
        zero = jnp.zeros_like(e)
        v = jnp.concatenate(
            [jnp.where(lane >= 224, e, zero), m, jnp.where(lane < 32, e, zero)], axis=0
        )
        high, low = high_low(v)
        return dot(oht3[k], high) + dot(oht3[k], low)

    def inner(x, _):
        yf[0, x] = spread(3, pg[x + 1, 0])
        yf[1, x] = spread(5, pg[x + 1, 9])
        for s in (0, 1):
            tz[s, x] = spread_z(3 + 2 * s, s, x + 1)
        return _

    lax.fori_loop(0, 8, inner, 0, unroll=UNROLL)
    for i, (u, x, ex) in enumerate(((0, 7, 0), (9, 0, 2))):
        def along(y, _, i=i, u=u, ex=ex):
            xf[i, y] = spread(3 * ex + 1, pg[u, y + 1])
            return _

        lax.fori_loop(0, 8, along, 0, unroll=UNROLL)
        yf[0, x] = yf[0, x] + spread(3 * ex, pg[u, 0])
        yf[1, x] = yf[1, x] + spread(3 * ex + 2, pg[u, 9])
        for s in (0, 1):
            tz[s, x] = tz[s, x] + spread_z(3 * ex + 2 * s, s, u)

    def own(x, _):
        for y in range(8):
            first, second = unpack_z(
                lambda h: tz[1, x, 0:64, h], lambda h: tz[0, x, 0:64, h], y, 64
            )
            extra = jnp.concatenate([first, second], axis=1)
            v = pg[x + 1, y + 1] + extra
            if y == 7:
                v = v + yf[0, x, 0:64, :]
            if y == 0:
                v = v + yf[1, x, 0:64, :]
            own_ref[8 * x + y] = v
        return _

    lax.fori_loop(0, 8, own, 0)
    for i, x in enumerate((7, 0)):
        for y in range(8):
            own_ref[8 * x + y] = own_ref[8 * x + y] + xf[i, y, 0:64, :]

    stores[5].start()

    def give(row, value):
        value = value.astype(BF16)
        for ref, order in ((to_left, (4, 7, 2)), (to_right, (3, 5, 0)), (below, (6,)), (above, (1,))):
            for i, d in enumerate(order):
                ref[row, 16 * i : 16 * i + 16, :] = value[16 * d : 16 * d + 16]

    far = slice(64, 192)
    for row, (x, y) in enumerate(SHELL):
        first, second = unpack_z(lambda h: tz[1, x, far, h], lambda h: tz[0, x, far, h], y, 128)
        v = jnp.concatenate([first, second], axis=1)
        if x in (0, 7):
            v = v + xf[0 if x == 7 else 1, y, far, :]
        if y in (0, 7):
            v = v + yf[0 if y == 7 else 1, x, far, :]
        give(row, v)
    for g in range(3):
        for k in range(3):
            parts = [
                squeeze(lambda p, hh: tz[p % 2, 1 + p // 2, far, halves(hh)], g, k, h, 128)
                for h in (0, 1)
            ]
            give(28 + 3 * g + k, jnp.concatenate(parts, axis=1))
    for c in stores:
        c.wait()


def dgrad(count, g_rows, wt, rows3, rows2):
    sd = jax.ShapeDtypeStruct
    return pl.pallas_call(
        dgrad_kernel,
        out_shape=[
            sd((64, 64, 256), F32),
            sd((256, 4096), BF16),
            sd((2, 256, 512), BF16),
            sd((9, 256, 256), BF16),
            sd((6, 256, 256), BF16),
            sd((6, 256, 256), BF16),
            sd((8, 256), F32),
        ]
        + [sd((ROWS, n, 256), BF16) for n in (48, 48, 16, 16)],
        in_specs=[SMEM] + [VMEM] * 4,
        out_specs=[ANY] * 6 + [VMEM] * 5,
        scratch_shapes=[
            pltpu.VMEM((64, 64, 256), F32),
            pltpu.VMEM((9, 256, 256), BF16),
            pltpu.VMEM((6, 256, 256), BF16),
            pltpu.VMEM((6, 256, 256), BF16),
            pltpu.VMEM((256, 4096), BF16),
            pltpu.VMEM((2, 256, 512), BF16),
            pltpu.VMEM((12, 8, 64, 256), BF16),
            pltpu.VMEM((2, 12, 64, 256), BF16),
            pltpu.VMEM((10, 10, 64, 256), F32),
            pltpu.VMEM((2, 10, 64, 256), F32),
            pltpu.VMEM((2, 10, 64, 256), F32),
            pltpu.VMEM((2, 8, 192, 256), F32),
            pltpu.VMEM((2, 8, 192, 256), F32),
            pltpu.VMEM((2, 8, 192, 256), F32),
            pltpu.VMEM((9, 192, 192), BF16),
            pltpu.VMEM((9, 192, 128), BF16),
            DMA((6,)),
        ],
        compiler_params=PARAMS,
        cost_estimate=cost(20000),
        name="dgrad",
    )(count, g_rows, wt, rows3, rows2)


def halo_kernel(fm_hbm, cols_ref, *refs):
    far_hbm, (vm_hbm, a_hbm, ax_hbm) = refs[:4], refs[4:7]
    fm_ref, vm_ref, a_ref, ax_ref = refs[7:11]
    fars, (xt, yt, tz, oh3, sems) = refs[11:15], refs[15:]
    from_left, from_right, from_below, from_above = fars
    loads = [
        pltpu.make_async_copy(src, dst, sems.at[i])
        for i, (src, dst) in enumerate(zip((fm_hbm, *far_hbm), (fm_ref, *fars)))
    ]
    for c in loads:
        c.start()
    ins = (
        (from_above, 0), (from_above, 16), (from_above, 32), (from_right, 0),
        (from_left, 0), (from_below, 0), (from_below, 16), (from_below, 32),
    )

    def imported(d, row, h=slice(None)):
        ref, at = ins[d]
        return ref[row, at : at + 16, h]

    far = slice(64, 192)
    tl = lanes(192, 192)
    for k in range(9):
        oh3[k] = one_hot(cols_ref[:, k : k + 1] == tl)
    loads[0].wait()

    def own_z(x, _):
        for s in (0, 1):
            parts = pack_z(lambda y, h: fm_ref[8 * x + y, :, h], s == 0, 64)
            tz[s, x, 0:64, :] = jnp.concatenate(parts, axis=1).astype(BF16)
        return _

    lax.fori_loop(0, 8, own_z, 0, unroll=2)
    for c in loads[1:5]:
        c.wait()
    for row, (x, y) in enumerate(SHELL):
        places = []
        if x in (0, 7):
            places.append((xt, 0 if x == 7 else 1, y))
        if y in (0, 7):
            places.append((yt, 0 if y == 7 else 1, x))
        for ref, i, j in places:
            ref[i, j, 0:64, :] = fm_ref[8 * x + y]
            for d in range(8):
                ref[i, j, 64 + 16 * d : 80 + 16 * d, :] = imported(d, row)
    for i, x in enumerate((7, 0)):
        for s in (0, 1):
            parts = pack_z(lambda y, h: xt[i, y, far, h], s == 0, 128)
            tz[s, x, far, :] = jnp.concatenate(parts, axis=1).astype(BF16)

    def compact(row, h):
        return jnp.concatenate([imported(d, 28 + row, halves(h)) for d in range(8)], axis=0).astype(F32)

    sub = lanes(128) // 32
    for x in range(1, 7):
        for s in (0, 1):
            top = s == 0
            src = halves(1 if top else 0)
            first = unsqueeze(compact, 2 * (x - 1) + s, 0, 128)
            second = unsqueeze(compact, 2 * (x - 1) + s, 1, 128)
            y0 = roll(yt[1, x, far, src].astype(F32), -96 if top else 0)
            y7 = roll(yt[0, x, far, src].astype(F32), 96 - (96 if top else 0))
            first = jnp.where(sub == 0, y0, first)
            second = jnp.where(sub == 3, y7, second)
            tz[s, x, far, :] = jnp.concatenate([first, second], axis=1).astype(BF16)

    lane = lanes(64, 256)

    def halo_z(k, s, x, u):
        v = dot(oh3[k], tz[s, x])
        zero = jnp.zeros((64, 256), F32)
        a_ref[s, u] = v[64:128].astype(BF16)
        ax_ref[s, u] = jnp.where(
            lane >= 224, v[0:64], jnp.where(lane < 32, v[128:192], zero)
        ).astype(BF16)

    def fill(x, _):
        for y in range(8):
            vm_ref[x + 1, y + 1] = fm_ref[8 * x + y]
        vm_ref[x + 1, 0] = dot(oh3[4, 0:64, :], yt[0, x]).astype(BF16)
        vm_ref[x + 1, 9] = dot(oh3[4, 128:192, :], yt[1, x]).astype(BF16)
        for s in (0, 1):
            halo_z(3 + 2 * s, s, x, x + 1)
        return _

    lax.fori_loop(0, 8, fill, 0, unroll=UNROLL)
    for i, (u, x, ex) in enumerate(((0, 7, 0), (9, 0, 2))):
        def along(y, _, i=i, u=u, ex=ex):
            vm_ref[u, y + 1] = dot(oh3[3 * ex + 1, 64:128, :], xt[i, y]).astype(BF16)
            return _

        lax.fori_loop(0, 8, along, 0, unroll=UNROLL)
        vm_ref[u, 0] = dot(oh3[3 * ex + 1, 0:64, :], xt[i, 7]).astype(BF16)
        vm_ref[u, 9] = dot(oh3[3 * ex + 1, 128:192, :], xt[i, 0]).astype(BF16)
        for s in (0, 1):
            halo_z(3 * ex + 2 * s, s, x, u)

    stores = [
        pltpu.make_async_copy(src, dst, sems.at[5 + i])
        for i, (src, dst) in enumerate(zip((vm_ref, a_ref, ax_ref), (vm_hbm, a_hbm, ax_hbm)))
    ]
    for c in stores:
        c.start()
    for c in stores:
        c.wait()


def halo(fm, cols3, arrived):
    sd = jax.ShapeDtypeStruct
    edges = [(10, 10, 64, 256), (2, 10, 64, 256), (2, 10, 64, 256)]
    return pl.pallas_call(
        halo_kernel,
        out_shape=[sd(v, BF16) for v in edges],
        in_specs=[ANY, VMEM] + [ANY] * 4,
        out_specs=[ANY] * 3,
        scratch_shapes=[pltpu.VMEM(v, BF16) for v in [fm.shape, *edges, *(v.shape for v in arrived)]]
        + [pltpu.VMEM((2, 8, 192, 256), BF16)] * 3
        + [pltpu.VMEM((9, 192, 192), BF16), DMA((8,))],
        compiler_params=PARAMS,
        cost_estimate=cost(1),
        name="halo",
    )(fm, cols3, *arrived)


def wgrad_kernel(*refs):
    hbm, bias_ref, dw_ref = refs[:5], refs[5], refs[6]
    vm_ref, a_ref, ax_ref, gm_ref, gz_ref = refs[7:12]
    acc, fold, sems = refs[12:]
    loads = [
        pltpu.make_async_copy(src, dst, sems.at[i])
        for i, (src, dst) in enumerate(zip(hbm, refs[7:12]))
    ]
    for c in loads:
        c.start()
    for c in (loads[0], loads[3]):
        c.wait()

    def tap(k, _):
        cols = vm_ref[pl.ds(k // 3, 8), pl.ds(k % 3, 8)].reshape(4096, 256)
        acc[k] = dot(gm_ref[...], cols)
        return _

    lax.fori_loop(0, 9, tap, 0, unroll=3)
    for c in (loads[1], loads[2], loads[4]):
        c.wait()
    for s in (0, 1):
        for a in range(3):
            for i, r in enumerate((a_ref, ax_ref)):
                acc[9 + 6 * s + 2 * a + i] = dot(gz_ref[s], r[s, a : a + 8].reshape(512, 256))

    blk = lanes(32, 256) // 32

    def band_sum(k, r):
        total = None
        for i in range(8):
            if not 0 <= i + r - 1 < 8:
                continue
            v = acc[k, 32 * i : 32 * i + 32, :]
            v = jnp.where(blk == i + r - 1, v, jnp.zeros_like(v))
            total = v if total is None else total + v
        return total

    def fold_lanes(total):
        v = total[:, 0:128] + total[:, 128:256]
        v = v + pltpu.roll(v, 64, axis=1)
        return v + pltpu.roll(v, 32, axis=1)

    for a in range(3):
        for q in range(3):
            for r in range(3):
                total = band_sum(3 * a + q, r)
                if r != 1:
                    s = r // 2
                    base = 9 + 6 * s + 2 * a
                    total = total + band_sum(base, q)
                    if q == 0:
                        v = acc[base + 1, 0:32, :]
                        total = total + jnp.where(blk == 7, v, jnp.zeros_like(v))
                    if q == 2:
                        v = acc[base + 1, 224:256, :]
                        total = total + jnp.where(blk == 0, v, jnp.zeros_like(v))
                t = 9 * a + 3 * q + r
                fold[32 * t : 32 * t + 32, :] = fold_lanes(total)
    quarter = lanes(216) // 32
    v = fold[0:216, :]
    for k in range(1, 4):
        v = jnp.where(quarter == k, fold[216 * k : 216 * k + 216, :], v)
    dw_ref[0:216, :] = v
    dw_ref[216:224, :] = fold_lanes(bias_ref[...])


def wgrad(vm, a, ax, gm, gz, bias_sum):
    return pl.pallas_call(
        wgrad_kernel,
        out_shape=jax.ShapeDtypeStruct((224, 128), F32),
        in_specs=[ANY] * 5 + [VMEM],
        out_specs=VMEM,
        scratch_shapes=[pltpu.VMEM(v.shape, v.dtype) for v in (vm, a, ax, gm, gz)]
        + [pltpu.VMEM((21, 256, 256), F32), pltpu.VMEM((864, 128), F32), DMA((5,))],
        compiler_params=PARAMS,
        cost_estimate=cost(1),
        name="wgrad",
    )(vm, a, ax, gm, gz, bias_sum)


def forward_kernel(first, count_ref, vm_hbm, a_hbm, ax_hbm, bm_hbm, bym_hbm, bye_hbm, bias_ref, *refs):
    out_hbm, vm_ref, a_ref, ax_ref, bm_ref, bym_ref, bye_ref, es, os, ob, sems = refs[-11:]
    n = os.shape[0] // 8
    planes = pl.ds(first, n + 2)
    loads = [
        pltpu.make_async_copy(a_hbm.at[:, planes], a_ref, sems.at[0]),
        pltpu.make_async_copy(ax_hbm.at[:, planes], ax_ref, sems.at[1]),
        pltpu.make_async_copy(bym_hbm, bym_ref, sems.at[2]),
        pltpu.make_async_copy(bye_hbm, bye_ref, sems.at[3]),
        pltpu.make_async_copy(bm_hbm, bm_ref, sems.at[4]),
        pltpu.make_async_copy(vm_hbm.at[planes], vm_ref, sems.at[5]),
    ]
    for c in loads:
        c.start()
    count = count_ref[0, 0]
    live = (lax.broadcasted_iota(jnp.int32, (64, 256), 0) < count).astype(F32)
    for c in loads[:4]:
        c.wait()
    for s in (0, 1):
        total = None
        for a in range(3):
            for ref, band in ((a_ref, bym_ref), (ax_ref, bye_ref)):
                part = dot(ref[s, a : a + n].reshape(64 * n, 256), band[2 * a + s])
                total = part if total is None else total + part
        es[s] = total.reshape(n, 64, 256)
    bias = bias_ref[...]
    for c in loads[4:]:
        c.wait()

    def plane(x, _):
        cols = jnp.concatenate(
            [vm_ref[x + a, q : q + 8].reshape(512, 256) for a in range(3) for q in range(3)], axis=1
        )
        total = dot(cols, bm_ref[...].reshape(2304, 256)).reshape(8, 64, 256)
        for y in range(8):
            low, high = unpack_z(lambda h: es[0, x, :, h], lambda h: es[1, x, :, h], y, 64)
            v = total[y] + jnp.concatenate([low, high], axis=1) + bias
            os[8 * x + y] = (v * live).astype(BF16)
        return _

    def store(i):
        rows = pl.ds(16 * i + 8 * first, 16)
        return pltpu.make_async_copy(ob.at[:, pl.ds(16 * i, 16)], out_hbm.at[:, rows], sems.at[6 + i])

    def two(i, _):
        plane(2 * i, 0)
        plane(2 * i + 1, 0)
        ob[:, pl.ds(pl.multiple_of(16 * i, 16), 16), :] = jnp.transpose(
            os[pl.ds(pl.multiple_of(16 * i, 16), 16)], (1, 0, 2)
        )
        return _

    for i in range(n // 2):
        two(i, 0)
        store(i).start()
    for i in range(n // 2):
        store(i).wait()


def forward(first, n, count, vm, a, ax, bm, bym, bye, bias_row, before=None):
    more = [] if before is None else [before]
    return pl.pallas_call(
        functools.partial(forward_kernel, first),
        out_shape=jax.ShapeDtypeStruct((64, 64, 256), BF16),
        in_specs=[SMEM] + [ANY] * 6 + [VMEM] + [ANY] * len(more),
        out_specs=ANY,
        input_output_aliases={8: 0} if more else {},
        scratch_shapes=[
            pltpu.VMEM((n + 2, 10, 64, 256), BF16),
            pltpu.VMEM((2, n + 2, 64, 256), BF16),
            pltpu.VMEM((2, n + 2, 64, 256), BF16),
            pltpu.VMEM(bm.shape, BF16),
            pltpu.VMEM(bym.shape, BF16),
            pltpu.VMEM(bye.shape, BF16),
            pltpu.VMEM((2, n, 64, 256), F32),
            pltpu.VMEM((8 * n, 64, 256), BF16),
            pltpu.VMEM((64, 8 * n, 256), BF16),
            DMA((6 + n // 2,)),
        ],
        compiler_params=PARAMS,
        cost_estimate=cost(1),
        name="forward",
    )(count, vm, a, ax, bm, bym, bye, bias_row, *more)


def finish_kernel(count_ref, own_hbm, slots_ref, *refs):
    hbm, out_hbm, (zp, os, ob, own_ref) = refs[:4], refs[4], refs[5:9]
    far, sems = refs[9:13], refs[13]
    from_left, from_right, from_below, from_above = far
    loads = [
        pltpu.make_async_copy(src, dst, sems.at[i])
        for i, (src, dst) in enumerate(zip((*hbm, own_hbm), (*far, own_ref)))
    ]
    for c in loads:
        c.start()
    count = count_ref[0, 0]
    live = (lax.broadcasted_iota(jnp.int32, (64, 256), 0) < count).astype(F32)
    chosen = one_hot(slots_ref[...] == lax.broadcasted_iota(jnp.int32, (64, 128), 0))

    def back(row):
        return dot(
            chosen,
            jnp.concatenate(
                [from_below[row], from_left[row, 0:16], from_right[row, 0:16], from_above[row]],
                axis=0,
            ),
        )

    for c in loads:
        c.wait()
    for row, (x, y) in enumerate(SHELL):
        v = own_ref[8 * x + y] + back(row)
        os[8 * x + y] = (v * live).astype(BF16)
    for k in range(9):
        zp[k] = back(28 + k)

    def piece(x, s, h):
        return unsqueeze(lambda row, hh: zp[row, :, halves(hh)], 2 * (x - 1) + s, h, 64)

    for x in range(1, 7):
        parts = {(s, h): piece(x, s, h) for s in (0, 1) for h in (0, 1)}
        for y in range(1, 7):
            first, second = unpack_z(
                lambda h: parts[1, h.start // 128], lambda h: parts[0, h.start // 128], y, 64
            )
            v = own_ref[8 * x + y] + jnp.concatenate([first, second], axis=1)
            os[8 * x + y] = (v * live).astype(BF16)
    stores = []
    for i in range(4):
        rows = slice(16 * i, 16 * i + 16)
        ob[:, rows, :] = jnp.transpose(os[rows], (1, 0, 2))
        stores.append(pltpu.make_async_copy(ob.at[:, rows], out_hbm.at[:, rows], sems.at[5 + i]))
        stores[-1].start()
    for c in stores:
        c.wait()


def finish(count, own, slots_row, returned):
    return pl.pallas_call(
        finish_kernel,
        out_shape=jax.ShapeDtypeStruct((64, 64, 256), BF16),
        in_specs=[SMEM, ANY, VMEM] + [ANY] * 4,
        out_specs=ANY,
        scratch_shapes=[
            pltpu.VMEM((9, 64, 256), F32),
            pltpu.VMEM((64, 64, 256), BF16),
            pltpu.VMEM((64, 64, 256), BF16),
            pltpu.VMEM((64, 64, 256), F32),
        ]
        + [pltpu.VMEM(v.shape, BF16) for v in returned]
        + [DMA((9,))],
        compiler_params=PARAMS,
        cost_estimate=cost(5),
        name="finish",
    )(count, own, slots_row, *returned)


def shift(value, axis, by):
    n = lax.axis_size(axis)
    return lax.ppermute(value, axis, [(i, i + by) for i in range(n) if 0 <= i + by < n])


def group(*blocks):
    return jnp.concatenate(blocks, axis=1)


def sum_steps():
    def doubling(axis, n, by):
        return lambda v: v + lax.ppermute(v, axis, [(i, i ^ by) for i in range(n)])

    def fourfold(axis, n, by):
        def step(v):
            a, b, c = (lax.ppermute(v, axis, [(i, i ^ (k * by)) for i in range(n)]) for k in (1, 2, 3))
            return (v + a) + (b + c)

        return step

    found = []
    for axis in ("tile", "space"):
        n = lax.axis_size(axis)
        if n & (n - 1):
            found.append([functools.partial(lax.psum, axis_name=axis)])
        else:
            bits = n.bit_length() - 1
            found.append([])
            if bits % 2 or axis == "space":
                found[-1].append(doubling(axis, n, 1))
            k = len(found[-1])
            while k < bits:
                found[-1].append((doubling if k + 1 == bits else fourfold)(axis, n, 1 << k))
                k += 2
    near, across = found
    return near + across[1:], across[:1]


def local(features, weight, bias_vector, cotangent, counts, send_slots, neighbours):
    slots = send_slots[0, 0].reshape(1, 128)
    near = neighbours[0, 0]
    full = jnp.concatenate(
        [near[:, :13], jnp.full((64, 1), 192, jnp.int32), near[:, 13:]], axis=1
    ).reshape(64, 3, 3, 3)
    cols3 = jnp.transpose(full, (2, 0, 1, 3)).reshape(192, 9)
    rows3 = cols3.T
    rows2 = full[:, :, :, 1].reshape(64, 9).T
    rows2 = jnp.concatenate([rows2, rows2], axis=1)
    wt = jnp.tile(weight.reshape(27, 32, 32), (1, 1, 8))
    bias_row = jnp.tile(bias_vector, 8).reshape(1, 256)

    fm, right, left, down, up = pack(counts, features.reshape(64, 64, 256), slots.reshape(128, 1))
    from_left = shift(right, "tile", 1)
    from_right = shift(left, "tile", -1)
    go_up = group(from_right[:, 16:32], up, from_left[:, 16:32])
    go_down = group(from_right[:, 32:48], down, from_left[:, 32:48])
    go_up, go_down, cotangent = lax.optimization_barrier((go_up, go_down, cotangent))
    from_below = shift(go_up, "space", 1)
    from_above = shift(go_down, "space", -1)
    own, gm, gz, bm, bym, bye, bias_sum, to_left, to_right, below, above = dgrad(
        counts, cotangent.reshape(64, 64, 256), wt, rows3, rows2
    )
    back_right = shift(to_left, "tile", -1)
    back_left = shift(to_right, "tile", 1)
    vm, a, ax = halo(fm, cols3, (from_left, from_right, from_below, from_above))
    vm, back_left, back_right = lax.optimization_barrier((vm, back_left, back_right))
    go_down = group(back_left[:, 16:32], below, back_right[:, 16:32])
    go_up = group(back_left[:, 32:48], above, back_right[:, 32:48])
    go_down, go_up, vm = lax.optimization_barrier((go_down, go_up, vm))
    back_above = shift(go_down, "space", -1)
    back_below = shift(go_up, "space", 1)
    dw = wgrad(vm, a, ax, gm, gz, bias_sum)
    args = (counts, vm, a, ax, bm, bym, bye, bias_row)
    near, across = sum_steps()
    total = dw
    for step in near:
        total = step(total)
    out = forward(0, 8, *args)
    total, out, back_above, back_below = lax.optimization_barrier((total, out, back_above, back_below))
    grad_in = finish(counts, own, slots, (back_left, back_right, back_below, back_above))
    for step in across:
        total = step(total)
    scale = float(lax.axis_size("space") * lax.axis_size("tile") * 64 * 512) ** (-0.5)
    total = total * scale
    weight_grad = jnp.transpose(total[:216].reshape(216, 4, 32), (1, 0, 2)).reshape(27, 32, 32)
    weight_grad = jnp.transpose(weight_grad, (0, 2, 1)).reshape(3, 3, 3, 32, 32)
    bias_grad = jnp.sum(total[216:224, :32], axis=0)
    return out.reshape(features.shape), grad_in.reshape(features.shape), weight_grad, bias_grad


def solution(mesh):
    wide = P("space", "tile", None, None, None, None)
    return jax.shard_map(
        local,
        mesh=mesh,
        in_specs=(wide, P(), P(), wide, P("space", "tile"), P("space", "tile", None, None), P("space", "tile", None, None)),
        out_specs=(wide, wide, P(), P()),
        check_vma=False,
    )
```
